32 devices in a mesh: groups: 2 (over x), seq: 16 (over z, y, core).
Axes of the slice: x: 2, y: 2, z: 4, core: 2. Of those that a mesh axis runs over, the one named last changes fastest.
Arguments:
- atom_features: bfloat16 [4, 8192, 256], P('groups', 'seq'), parts along dimension 0, may hold values from -6 to 6
- cotangent: bfloat16 [4, 8192, 256], P('groups', 'seq'), parts along dimension 0, may hold values from -6 to 6
- charge_weight: bfloat16 [256, 16], replicated, may hold values from -0.375 to 0.375
- message_weight: bfloat16 [16, 256], replicated, may hold values from -1.5 to 1.5
- amplitude: float32 [16], replicated, may hold values from 1 to 4
- smoothing: float32 [16], replicated, may hold values from 0.5 to 2
- screening: float32 [16], replicated, may hold values from 0.05 to 0.15
- base_cells: int32 [4, 3, 8192], P('groups', None, 'seq'), parts along dimension 0, may hold values from 0 to 63, as said below
- cell_offsets: float32 [4, 3, 8192], P('groups', None, 'seq'), parts along dimension 0, may hold values from 0 to 1
- row_starts: int32 [4, 64], P('groups', 'seq'), parts along dimension 0, may hold values from 0 to 56, as said below
- block_counts: int32 [4, 64], P('groups', 'seq'), parts along dimension 0, may hold values from 1 to 128, 7168 in all within a row
Outputs:
- message: bfloat16 [4, 8192, 256], P('groups', 'seq'), parts along dimension 0
- atom_gradient: bfloat16 [4, 8192, 256], P('groups', 'seq'), parts along dimension 0
- gradient_in: float32 [512, 16], P('groups'), parts along dimension 0
- gradient_out: float32 [32, 256], P('groups'), parts along dimension 0
- filter_gradient: float32 [6, 16], P('groups'), parts along dimension 0
The draws below stay inside these ranges and needn't reach their ends.
There are 2 independent parts, one for each index of `groups`. The reference program is written for one: setup_inputs(seed, part) draws one part's arguments, and reference() takes and returns one part's arrays. A program takes and returns all parts, laid end to end along the dimension named above; an argument that names none is the same for every part. Nothing has to cross between parts.
Inputs may be any that keep to these rules, and one draw needn't show every extreme that they name: `base_cells`: an atom in block b held by seq index d (blocks d * 4 to (d + 1) * 4 - 1) has its depth base in [d * 4, (d + 1) * 4) and its row base equal to (row_starts of block b + r) mod 64 with 0 <= r <= 28; its column base is any cell. `row_starts`: each block's first brick row is a multiple of 8. `block_counts`: slots of a block below its count hold atoms, the others are padding.
All inputs are finite; a program needn't handle non-finite values.
Results may differ from the reference program's by a relative error of at most 0.0068.
Values may be sent and summed in bfloat16 or wider, within the bound.
A program may use at most 128 MiB of HBM per device.

```python
import math
import jax
import jax.numpy as jnp
import numpy as np
from jax import lax

D = 256
C = 16
M = 64
BAND = 32
BLOCK_ROWS = 128
BLOCKS = 4
CELLS = 2
ATOMS_DEV = 512
ATOMS = 8192
ALL_BLOCKS = 64
PLANES = 4


def shared_layout(key):
    key_levels, key_ranking, key_depth, key_rows, key_columns = jax.random.split(key, 5)
    levels = M // 8
    picked = jax.random.randint(key_levels, (CELLS, ALL_BLOCKS), 0, levels)
    ranking = jax.vmap(lambda cell_key: jax.random.permutation(cell_key, ALL_BLOCKS))(jax.random.split(key_ranking, CELLS))
    row_starts = 8 * jnp.where(ranking < levels, ranking, picked)
    device_of = jnp.arange(ATOMS, dtype=jnp.int32) // ATOMS_DEV
    block_of = jnp.arange(ATOMS, dtype=jnp.int32) // BLOCK_ROWS
    depth_base = device_of[None, :] * PLANES + jax.random.randint(key_depth, (CELLS, ATOMS), 0, PLANES)
    row_base = (jnp.take(row_starts, block_of, axis=1) + jax.random.randint(key_rows, (CELLS, ATOMS), 0, BAND - 3)) % M
    column_base = jax.random.randint(key_columns, (CELLS, ATOMS), 0, M)
    return (row_starts.astype(jnp.int32), jnp.stack([depth_base, row_base, column_base], axis=1).astype(jnp.int32))


def draw_base_cells(key, part):
    layout = shared_layout(key)
    return layout[1]


def draw_row_starts(key, part):
    layout = shared_layout(key)
    return layout[0]


def steps_of(own_key, shape, cuts, smallest, high):
    factor_of = 1.0
    for dim, parts in cuts:
        heights = jax.random.uniform(jax.random.fold_in(jax.random.fold_in(own_key, 6), dim), (parts,), jnp.float32, smallest / len(cuts), high / len(cuts))
        factor_of = factor_of * jnp.repeat(jnp.exp(heights), shape[dim] // parts).reshape((-1,) + (1,) * (len(shape) - 1 - dim))
    return factor_of


def split_up(count, total, most, skew):
    portions = [(1 << 20) // math.isqrt(standing ** skew) + 1 for standing in range(2, count + 1)]
    rest, holding = total - most - (count - 1), [1] * (count - 1)
    while rest > 0:
        free = [i for i in range(count - 1) if holding[i] < most]
        mass, left = sum([portions[i] for i in free]), rest
        for i in free:
            extra = min(most - holding[i], max(1, left * portions[i] // mass), rest)
            holding[i] = holding[i] + extra
            rest = rest - extra
    return np.array([most] + holding)


def ragged_sizes(own_key, amount, total, limit, lean):
    if amount == 2:
        one = jax.random.randint(own_key, (), max(1, total - limit), min(limit, total - 1) + 1)
        return jnp.stack([one, total - one])
    sizes = jnp.asarray(split_up(amount, total, limit, lean), jnp.int32)
    twos = (amount - 1) // 2
    giver, sink = sizes[1:1 + 2 * twos:2], sizes[2:2 + 2 * twos:2]
    room = jnp.minimum(giver - 1, limit - sink)
    passed = jax.random.randint(jax.random.fold_in(own_key, 1), (twos,), 0, 1 << 20) % (room + 1)
    sizes = sizes.at[1:1 + 2 * twos:2].set(giver - passed).at[2:2 + 2 * twos:2].set(sink + passed)
    return sizes[jax.random.permutation(jax.random.fold_in(own_key, 2), amount)]


def bell_draw(own_key, dims, width, limit, pieces=(), kind=jnp.bfloat16):
    values = width * jax.random.normal(own_key, dims, jnp.float32)
    if pieces:
        values = values * steps_of(own_key, dims, pieces, -0.22, 0.18)
    return jnp.clip(values, -limit, limit).astype(kind)


def setup_inputs(seed: int = 0, part: int = 0) -> dict:
    splits = jax.random.split(jax.random.key(seed), 12)
    part_keys = jax.random.split(jax.random.fold_in(splits[11], part), 12)
    atom_features = bell_draw(part_keys[0], (CELLS, ATOMS, D), 1.0, 6.0, ((1, 16),))
    cotangent = bell_draw(part_keys[1], (CELLS, ATOMS, D), 1.0, 6.0, ((1, 16),))
    charge_weight = bell_draw(splits[2], (D, C), D ** -0.5, 0.375)
    message_weight = bell_draw(splits[3], (C, D), C ** -0.5, 1.5)
    amplitude = jnp.clip(jnp.exp(jax.random.uniform(splits[4], (C,), jnp.float32, math.log(1.0), math.log(4.0))), 1.0, 4.0)
    smoothing = jnp.clip(jnp.exp(jax.random.uniform(splits[5], (C,), jnp.float32, math.log(0.5), math.log(2.0))), 0.5, 2.0)
    screening = jnp.clip(jnp.exp(jax.random.uniform(splits[6], (C,), jnp.float32, math.log(0.05), math.log(0.15))), 0.05, 0.15)
    base_cells = draw_base_cells(jax.random.fold_in(jax.random.fold_in(splits[11], part), 71), part)
    cell_offsets = jnp.clip(1.0 * jax.random.uniform(part_keys[8], (CELLS, 3, ATOMS), jnp.float32) ** steps_of(part_keys[8], (CELLS, 3, ATOMS), ((2, 16),), -0.2, 0.2), 0.0, 1.0)
    row_starts = draw_row_starts(jax.random.fold_in(jax.random.fold_in(splits[11], part), 71), part)
    block_counts = jax.vmap(lambda own: ragged_sizes(own, ALL_BLOCKS, ALL_BLOCKS * BLOCK_ROWS * 7 // 8, BLOCK_ROWS, 1))(jax.random.split(part_keys[10], CELLS)).reshape((CELLS, ALL_BLOCKS)).astype(jnp.int32)
    return {"atom_features": atom_features, "cotangent": cotangent, "charge_weight": charge_weight, "message_weight": message_weight, "amplitude": amplitude, "smoothing": smoothing, "screening": screening, "base_cells": base_cells, "cell_offsets": cell_offsets, "row_starts": row_starts, "block_counts": block_counts}


def spline_weights(fraction):
    remain = 1.0 - fraction
    square = fraction * fraction
    cubed = square * fraction
    return (remain * remain * remain / 6.0, (3.0 * cubed - 6.0 * square + 4.0) / 6.0, (-3.0 * cubed + 3.0 * square + 3.0 * fraction + 1.0) / 6.0, cubed / 6.0)

def pick_weight(lattice_gap, weights):
    picked = jnp.where(lattice_gap == 0, weights[0], 0.0)
    for order_index in range(1, 4):
        picked = picked + jnp.where(lattice_gap == order_index, weights[order_index], 0.0)
    return picked

def atom_weights(base_cells, cell_offsets, row_start, plane_start, plane_count):
    atom_count = base_cells.shape[1]
    depth_index = plane_start + jnp.arange(plane_count, dtype=jnp.int32)
    row_index = row_start + jnp.arange(BAND, dtype=jnp.int32)
    column_index = jnp.arange(M, dtype=jnp.int32)
    along_depth = pick_weight((depth_index[None, :] - base_cells[0][:, None]) % M, spline_weights(cell_offsets[0][:, None]))
    along_rows = pick_weight((row_index[None, :] - base_cells[1][:, None]) % M, spline_weights(cell_offsets[1][:, None]))
    along_columns = pick_weight((column_index[None, :] - base_cells[2][:, None]) % M, spline_weights(cell_offsets[2][:, None]))
    plane_rows = (along_depth[:, :, None] * along_rows[:, None, :]).reshape(atom_count, plane_count * BAND).astype(jnp.bfloat16)
    return (plane_rows, along_columns)

def hartley_table():
    indices = jnp.arange(M, dtype=jnp.int32)
    product = indices[:, None] * indices[None, :] % M
    angles = product.astype(jnp.float32) * (2.0 * math.pi / M)
    return jnp.cos(angles) + jnp.sin(angles)

def wave_numbers(indices):
    return jnp.where(indices < M // 2, indices, indices - M).astype(jnp.float32) * (2.0 * math.pi / M)

def squared_waves(row_first, row_count):
    depth_waves = wave_numbers(jnp.arange(M, dtype=jnp.int32))
    row_waves = wave_numbers(row_first + jnp.arange(row_count, dtype=jnp.int32))
    summed = depth_waves[:, None, None] ** 2 + row_waves[None, :, None] ** 2 + depth_waves[None, None, :] ** 2
    return summed[:, :, None, :]

def scaled_filter(amplitude, smoothing, screening, wave_square):
    gains = amplitude[None, None, :, None]
    widths = (smoothing * smoothing)[None, None, :, None]
    screens = (screening * screening)[None, None, :, None]
    return gains * jnp.exp(-0.5 * widths * wave_square) / (wave_square + screens) * (1.0 / M ** 3)

def forward_transform(mesh):
    hartley = hartley_table()
    highest = lax.Precision.HIGHEST
    mesh = jnp.einsum('zycx,xf->zycf', mesh, hartley, precision=highest)
    mesh = jnp.einsum('zycx,yf->zfcx', mesh, hartley, precision=highest)
    return jnp.einsum('zycx,zf->fycx', mesh, hartley, precision=highest)

def inverse_transform(spectrum):
    hartley = hartley_table()
    highest = lax.Precision.HIGHEST
    spectrum = jnp.einsum('zycx,zf->fycx', spectrum, hartley, precision=highest)
    spectrum = jnp.einsum('zycx,yf->zfcx', spectrum, hartley, precision=highest)
    return jnp.einsum('zycx,xf->zycf', spectrum, hartley, precision=highest)

def spread_global(charges, base_cells, cell_offsets, row_starts):
    columns = C * M
    extent = PLANES + 3
    zero = jnp.zeros((), jnp.int32)

    def add_block(padded, block_index):
        first_row = block_index * BLOCK_ROWS
        block_charges = lax.dynamic_slice_in_dim(charges, first_row, BLOCK_ROWS, 0)
        block_cells = lax.dynamic_slice_in_dim(base_cells, first_row, BLOCK_ROWS, 1)
        block_offsets = lax.dynamic_slice_in_dim(cell_offsets, first_row, BLOCK_ROWS, 1)
        row_start = row_starts[block_index].astype(jnp.int32)
        plane_start = (block_index // BLOCKS * PLANES).astype(jnp.int32)
        plane_rows, along_columns = atom_weights(block_cells, block_offsets, row_start, plane_start, extent)
        spread_rows = (block_charges.astype(jnp.float32)[:, :, None] * along_columns[:, None, :]).reshape(BLOCK_ROWS, columns).astype(jnp.bfloat16)
        addition = jnp.dot(plane_rows.T, spread_rows, preferred_element_type=jnp.float32).reshape(extent, BAND, columns)
        current = lax.dynamic_slice(padded, (plane_start, row_start, zero), (extent, BAND, columns))
        return (lax.dynamic_update_slice(padded, current + addition, (plane_start, row_start, zero)), None)
    padded = jnp.zeros((M + 3, M + BAND, columns), jnp.float32)
    padded, unused = lax.scan(add_block, padded, jnp.arange(ALL_BLOCKS, dtype=jnp.int32))
    folded = padded[:M].at[:3].add(padded[M:])
    return folded[:, :M].at[:, :BAND].add(folded[:, M:])

def interpolate_global(mesh, base_cells, cell_offsets, row_starts):
    columns = C * M
    extent = PLANES + 3
    zero = jnp.zeros((), jnp.int32)
    padded = jnp.concatenate([mesh, mesh[:3]], axis=0)
    padded = jnp.concatenate([padded, padded[:, :BAND]], axis=1)

    def one_block(block_index):
        first_row = block_index * BLOCK_ROWS
        block_cells = lax.dynamic_slice_in_dim(base_cells, first_row, BLOCK_ROWS, 1)
        block_offsets = lax.dynamic_slice_in_dim(cell_offsets, first_row, BLOCK_ROWS, 1)
        row_start = row_starts[block_index].astype(jnp.int32)
        plane_start = (block_index // BLOCKS * PLANES).astype(jnp.int32)
        plane_rows, along_columns = atom_weights(block_cells, block_offsets, row_start, plane_start, extent)
        window = lax.dynamic_slice(padded, (plane_start, row_start, zero), (extent, BAND, columns)).reshape(extent * BAND, columns)
        values = jnp.dot(plane_rows, window, preferred_element_type=jnp.float32)
        return lax.optimization_barrier(jnp.sum(values.reshape(BLOCK_ROWS, C, M) * along_columns[:, None, :], axis=2))
    return lax.map(one_block, jnp.arange(ALL_BLOCKS, dtype=jnp.int32)).reshape(ATOMS, C)

def reference(atom_features, cotangent, charge_weight, message_weight, amplitude, smoothing, screening, base_cells, cell_offsets, row_starts, block_counts):
    live_mask = (jnp.arange(BLOCK_ROWS, dtype=jnp.int32)[None, None, :] < block_counts[:, :, None]).reshape(CELLS, ATOMS).astype(jnp.float32)
    flat_atoms = atom_features.reshape(CELLS * ATOMS, D)
    flat_cotangent = cotangent.reshape(CELLS * ATOMS, D)
    projected = jnp.dot(flat_atoms, charge_weight, preferred_element_type=jnp.float32).reshape(CELLS, ATOMS, C)
    charges = (live_mask[:, :, None] * projected).astype(jnp.bfloat16)
    pulled = jnp.dot(flat_cotangent, message_weight.T, preferred_element_type=jnp.float32).reshape(CELLS, ATOMS, C)
    adjoint = (live_mask[:, :, None] * pulled).astype(jnp.bfloat16)
    wave_square = squared_waves(jnp.zeros((), jnp.int32), M)
    spectral_filter = scaled_filter(amplitude, smoothing, screening, wave_square)

    def one_cell(cell_data):
        source_spectrum = forward_transform(spread_global(cell_data[0], cell_data[2], cell_data[3], cell_data[4]).reshape(M, M, C, M))
        adjoint_spectrum = forward_transform(spread_global(cell_data[1], cell_data[2], cell_data[3], cell_data[4]).reshape(M, M, C, M))
        potential_mesh = inverse_transform(spectral_filter * source_spectrum).reshape(M, M, C * M).astype(jnp.bfloat16)
        response_mesh = inverse_transform(spectral_filter * adjoint_spectrum).reshape(M, M, C * M).astype(jnp.bfloat16)
        potential = interpolate_global(potential_mesh, cell_data[2], cell_data[3], cell_data[4])
        response = interpolate_global(response_mesh, cell_data[2], cell_data[3], cell_data[4])
        return (potential, response, source_spectrum * adjoint_spectrum)
    potential, response, products = lax.map(one_cell, (charges, adjoint, base_cells, cell_offsets, row_starts))
    potential_rounded = potential.astype(jnp.bfloat16)
    message = (live_mask[:, :, None] * jnp.dot(potential_rounded.reshape(-1, C), message_weight, preferred_element_type=jnp.float32).reshape(CELLS, ATOMS, D)).astype(jnp.bfloat16)
    response_rounded = (live_mask[:, :, None] * response).astype(jnp.bfloat16)
    atom_gradient = jnp.dot(response_rounded.reshape(-1, C), charge_weight.T, preferred_element_type=jnp.float32).reshape(CELLS, ATOMS, D).astype(jnp.bfloat16)
    gradient_scale = 1.0 / math.sqrt(CELLS * ATOMS)
    masked_cotangent = jnp.where(live_mask[:, :, None] > 0, cotangent, jnp.zeros((), jnp.bfloat16))
    gradient_in = jnp.dot(flat_atoms.T, response_rounded.reshape(-1, C), preferred_element_type=jnp.float32) * gradient_scale
    gradient_out = jnp.dot(potential_rounded.reshape(-1, C).T, masked_cotangent.reshape(-1, D), preferred_element_type=jnp.float32) * gradient_scale
    intersection = lax.optimization_barrier(jnp.sum(products, axis=0)) * spectral_filter
    widths = (smoothing * smoothing)[None, None, :, None]
    screens = (screening * screening)[None, None, :, None]
    smooth_factor = -widths * wave_square
    screen_factor = -2.0 * screens / (wave_square + screens)
    filter_gradient = jnp.stack([lax.optimization_barrier(jnp.sum(intersection, axis=(0, 1, 3))), lax.optimization_barrier(jnp.sum(intersection * smooth_factor, axis=(0, 1, 3))), lax.optimization_barrier(jnp.sum(intersection * screen_factor, axis=(0, 1, 3)))]) * gradient_scale
    return (message, atom_gradient, gradient_in, gradient_out, filter_gradient)
```

```python
import functools
import math

import jax
import jax.numpy as jnp
import ml_dtypes
import numpy as np
from jax import lax
from jax.experimental import pallas as pl
from jax.experimental.pallas import tpu as pltpu
from jax.sharding import PartitionSpec as P

M = 64
BAND = 32


def passed_along(value, axis, by):
    count = lax.axis_size(axis)
    return lax.ppermute(value, axis, [(i, (i + by) % count) for i in range(count)])


def spline_weights(fraction):
    remain = 1.0 - fraction
    square = fraction * fraction
    cubed = square * fraction
    return (
        remain * remain * remain / 6.0,
        (3.0 * cubed - 6.0 * square + 4.0) / 6.0,
        (-3.0 * cubed + 3.0 * square + 3.0 * fraction + 1.0) / 6.0,
        cubed / 6.0,
    )


def pick_weight(lattice_gap, weights):
    picked = jnp.where(lattice_gap == 0, weights[0], 0.0)
    for order_index in range(1, 4):
        picked = picked + jnp.where(lattice_gap == order_index, weights[order_index], 0.0)
    return picked


def atom_weights(base_cells, cell_offsets, row_start, plane_start, plane_count):
    atom_count = base_cells.shape[1]
    depth_index = plane_start + jnp.arange(plane_count, dtype=jnp.int32)
    row_index = row_start + jnp.arange(BAND, dtype=jnp.int32)
    column_index = jnp.arange(M, dtype=jnp.int32)
    along_depth = pick_weight(
        (depth_index[None, :] - base_cells[0][:, None]) % M,
        spline_weights(cell_offsets[0][:, None]),
    )
    along_rows = pick_weight(
        (row_index[None, :] - base_cells[1][:, None]) % M, spline_weights(cell_offsets[1][:, None])
    )
    along_columns = pick_weight(
        (column_index[None, :] - base_cells[2][:, None]) % M,
        spline_weights(cell_offsets[2][:, None]),
    )
    plane_rows = (
        (along_depth[:, :, None] * along_rows[:, None, :])
        .reshape(atom_count, plane_count * BAND)
        .astype(jnp.bfloat16)
    )
    return (plane_rows, along_columns)


def hartley_table():
    indices = jnp.arange(M, dtype=jnp.int32)
    product = indices[:, None] * indices[None, :] % M
    angles = product.astype(jnp.float32) * (2.0 * math.pi / M)
    return jnp.cos(angles) + jnp.sin(angles)


def wave_numbers(indices):
    return jnp.where(indices < M // 2, indices, indices - M).astype(jnp.float32) * (
        2.0 * math.pi / M
    )


def squared_waves(row_first, row_count):
    depth_waves = wave_numbers(jnp.arange(M, dtype=jnp.int32))
    row_waves = wave_numbers(row_first + jnp.arange(row_count, dtype=jnp.int32))
    summed = (
        depth_waves[:, None, None] ** 2
        + row_waves[None, :, None] ** 2
        + depth_waves[None, None, :] ** 2
    )
    return summed[:, :, None, :]


def scaled_filter(amplitude, smoothing, screening, wave_square):
    gains = amplitude[None, None, :, None]
    widths = (smoothing * smoothing)[None, None, :, None]
    screens = (screening * screening)[None, None, :, None]
    return gains * jnp.exp(-0.5 * widths * wave_square) / (wave_square + screens) * (1.0 / M**3)


def spread_cell(charges, base_cells, cell_offsets, row_starts, plane_start, plane_count):
    blocks = row_starts.shape[0]
    atom_count = charges.shape[0] // blocks
    columns = charges.shape[1] * M

    def add_block(padded, block_index):
        first_row = block_index * atom_count
        block_charges = lax.dynamic_slice_in_dim(charges, first_row, atom_count, 0)
        block_cells = lax.dynamic_slice_in_dim(base_cells, first_row, atom_count, 1)
        block_offsets = lax.dynamic_slice_in_dim(cell_offsets, first_row, atom_count, 1)
        row_start = row_starts[block_index]
        plane_rows, along_columns = atom_weights(
            block_cells, block_offsets, row_start, plane_start, plane_count
        )
        spread_rows = (
            (block_charges.astype(jnp.float32)[:, :, None] * along_columns[:, None, :])
            .reshape(atom_count, columns)
            .astype(jnp.bfloat16)
        )
        addition = lax.dot_general(
            plane_rows, spread_rows, (((0,), (0,)), ((), ())), preferred_element_type=jnp.float32
        )
        addition = addition.reshape(plane_count, BAND, columns)
        current = lax.dynamic_slice_in_dim(padded, row_start, BAND, 1)
        return (lax.dynamic_update_slice_in_dim(padded, current + addition, row_start, 1), None)

    padded = jnp.zeros((plane_count, M + BAND, columns), jnp.float32)
    padded, unused = lax.scan(add_block, padded, jnp.arange(blocks, dtype=jnp.int32))
    return padded[:, :M].at[:, :BAND].add(padded[:, M:])


def interpolate_cell(mesh, base_cells, cell_offsets, row_starts, plane_start):
    plane_count = mesh.shape[0]
    blocks = row_starts.shape[0]
    atom_count = base_cells.shape[1] // blocks
    padded = jnp.concatenate([mesh, mesh[:, :BAND]], axis=1)

    def one_block(block_index):
        first_row = block_index * atom_count
        block_cells = lax.dynamic_slice_in_dim(base_cells, first_row, atom_count, 1)
        block_offsets = lax.dynamic_slice_in_dim(cell_offsets, first_row, atom_count, 1)
        row_start = row_starts[block_index]
        plane_rows, along_columns = atom_weights(
            block_cells, block_offsets, row_start, plane_start, plane_count
        )
        window = lax.dynamic_slice_in_dim(padded, row_start, BAND, 1).reshape(
            plane_count * BAND, -1
        )
        values = jnp.dot(plane_rows, window, preferred_element_type=jnp.float32)
        return jnp.sum(values.reshape(atom_count, -1, M) * along_columns[:, None, :], axis=2)

    return lax.map(one_block, jnp.arange(blocks, dtype=jnp.int32)).reshape(blocks * atom_count, -1)


def spread_cells(charges, base_cells, cell_offsets, row_starts, plane_start, plane_count):

    def spread_one_cell(cell_data):
        return spread_cell(
            cell_data[0], cell_data[1], cell_data[2], cell_data[3], plane_start, plane_count
        )

    return lax.map(spread_one_cell, (charges, base_cells, cell_offsets, row_starts))


def interpolate_cells(mesh, base_cells, cell_offsets, row_starts, plane_start):

    def interpolate_one_cell(cell_data):
        return interpolate_cell(cell_data[0], cell_data[1], cell_data[2], cell_data[3], plane_start)

    return lax.map(interpolate_one_cell, (mesh, base_cells, cell_offsets, row_starts))


def long_range(charges, base_cells, cell_offsets, row_starts, spectral_filter):
    devices = lax.axis_size("seq")
    planes = M // devices
    spill_reach = (planes + 2) // planes
    plane_start = lax.axis_index("seq") * planes
    cell_count = charges.shape[0]
    channels = charges.shape[2]
    hartley = hartley_table()
    highest = lax.Precision.HIGHEST
    extended = spread_cells(charges, base_cells, cell_offsets, row_starts, plane_start, planes + 3)
    mesh_field = extended[:, :planes]
    for distance in range(1, spill_reach + 1):
        lower_plane = (distance - 1) * planes
        upper_plane = min(distance * planes, 3)
        arrived = passed_along(
            extended[:, planes + lower_plane : planes + upper_plane], "seq", distance
        )
        mesh_field = mesh_field.at[:, : upper_plane - lower_plane].add(arrived)
    slab_data = mesh_field.reshape(cell_count, planes, M, channels, M)
    spectrum = jnp.einsum("kpycx,xf->kpycf", slab_data, hartley, precision=highest)
    spectrum = jnp.einsum("kpycx,yf->kpfcx", spectrum, hartley, precision=highest)
    forward = jnp.einsum(
        "kzycx,zf->kfycx",
        lax.all_to_all(spectrum, "seq", split_axis=2, concat_axis=1, tiled=True),
        hartley,
        precision=highest,
    )
    weighted = spectral_filter[None] * forward
    returned = jnp.einsum("kzycx,zf->kfycx", weighted, hartley, precision=highest)
    slab_back = lax.all_to_all(returned, "seq", split_axis=1, concat_axis=2, tiled=True)
    slab_back = jnp.einsum("kpycx,yf->kpfcx", slab_back, hartley, precision=highest)
    slab_back = jnp.einsum("kpycx,xf->kpycf", slab_back, hartley, precision=highest)
    rounded = slab_back.reshape(cell_count, planes, M, channels * M).astype(jnp.bfloat16)
    pieces = [rounded]
    for distance in range(1, spill_reach + 1):
        lower_plane = (distance - 1) * planes
        upper_plane = min(distance * planes, 3)
        pieces.append(passed_along(rounded[:, : upper_plane - lower_plane], "seq", -distance))
    values = interpolate_cells(
        jnp.concatenate(pieces, axis=1), base_cells, cell_offsets, row_starts, plane_start
    )
    return (values, forward)


def on_device(
    atom_features,
    cotangent,
    charge_weight,
    message_weight,
    amplitude,
    smoothing,
    screening,
    base_cells,
    cell_offsets,
    row_starts,
    block_counts,
):
    cell_count, atom_rows, features = atom_features.shape
    channels = charge_weight.shape[1]
    devices = lax.axis_size("seq")
    blocks = block_counts.shape[1]
    slot_index = jnp.arange(atom_rows // blocks, dtype=jnp.int32)
    live_mask = (
        (slot_index[None, None, :] < block_counts[:, :, None])
        .reshape(cell_count, atom_rows)
        .astype(jnp.float32)
    )
    projected = jnp.dot(
        atom_features.reshape(-1, features), charge_weight, preferred_element_type=jnp.float32
    )
    charges = (live_mask[:, :, None] * projected.reshape(cell_count, atom_rows, channels)).astype(
        jnp.bfloat16
    )
    pulled = lax.dot_general(
        cotangent.reshape(-1, features),
        message_weight,
        (((1,), (1,)), ((), ())),
        preferred_element_type=jnp.float32,
    )
    adjoint = (live_mask[:, :, None] * pulled.reshape(cell_count, atom_rows, channels)).astype(
        jnp.bfloat16
    )
    row_count = M // devices
    wave_square = squared_waves(lax.axis_index("seq") * row_count, row_count)
    spectral_filter = scaled_filter(amplitude, smoothing, screening, wave_square)
    potential, source_spectra = long_range(
        charges, base_cells, cell_offsets, row_starts, spectral_filter
    )
    response, adjoint_spectra = long_range(
        adjoint, base_cells, cell_offsets, row_starts, spectral_filter
    )
    potential_rounded = potential.astype(jnp.bfloat16)
    outgoing = jnp.dot(
        potential_rounded.reshape(-1, channels), message_weight, preferred_element_type=jnp.float32
    )
    message = (live_mask[:, :, None] * outgoing.reshape(cell_count, atom_rows, features)).astype(
        jnp.bfloat16
    )
    response_rounded = (live_mask[:, :, None] * response).astype(jnp.bfloat16)
    backward = lax.dot_general(
        response_rounded.reshape(-1, channels),
        charge_weight,
        (((1,), (1,)), ((), ())),
        preferred_element_type=jnp.float32,
    )
    atom_gradient = backward.reshape(cell_count, atom_rows, features).astype(jnp.bfloat16)
    gradient_scale = 1.0 / math.sqrt(cell_count * atom_rows * devices)
    masked_cotangent = jnp.where(live_mask[:, :, None] > 0, cotangent, jnp.zeros((), jnp.bfloat16))
    gradient_in = (
        lax.dot_general(
            atom_features.reshape(-1, features),
            response_rounded.reshape(-1, channels),
            (((0,), (0,)), ((), ())),
            preferred_element_type=jnp.float32,
        )
        * gradient_scale
    )
    gradient_out = (
        lax.dot_general(
            potential_rounded.reshape(-1, channels),
            masked_cotangent.reshape(-1, features),
            (((0,), (0,)), ((), ())),
            preferred_element_type=jnp.float32,
        )
        * gradient_scale
    )
    intersection = jnp.sum(source_spectra * adjoint_spectra, axis=0) * spectral_filter
    widths = (smoothing * smoothing)[None, None, :, None]
    screens = (screening * screening)[None, None, :, None]
    smooth_factor = -widths * wave_square
    screen_factor = -2.0 * screens / (wave_square + screens)
    filter_terms = (
        jnp.stack(
            [
                jnp.sum(intersection, axis=(0, 1, 3)),
                jnp.sum(intersection * smooth_factor, axis=(0, 1, 3)),
                jnp.sum(intersection * screen_factor, axis=(0, 1, 3)),
            ]
        )
        * gradient_scale
    )
    gradient_in, gradient_out, filter_terms = lax.psum(
        (gradient_in, gradient_out, filter_terms), "seq"
    )
    return (message, atom_gradient, gradient_in, gradient_out, filter_terms)


def stacked_tables(planes):
    indices = np.arange(M)
    angles = (indices[:, None] * indices[None, :] % M) * (2.0 * np.pi / M)
    hartley = (np.cos(angles) + np.sin(angles)).astype(np.float32)
    window = (np.arange(M // planes)[:, None] * planes + np.arange(8)[None, :]) % M
    depth = hartley[:, window.reshape(-1)]

    def parts(table):
        high = table.astype(ml_dtypes.bfloat16)
        low = (table - high.astype(np.float32)).astype(ml_dtypes.bfloat16)
        return jnp.asarray(np.concatenate([high, high, low], axis=1))

    return (parts(hartley), parts(depth), parts(depth.T))


def stacked_parts(value):
    high = value.astype(jnp.bfloat16)
    low = (value - high.astype(jnp.float32)).astype(jnp.bfloat16)
    return jnp.concatenate([high, low, high], axis=0)


def wave_squares(indices):
    waves = jnp.where(indices < M // 2, indices, indices - M).astype(jnp.float32)
    return waves * waves * ((2.0 * math.pi / M) ** 2)


def mesh_kernel(
    planes,
    params_ref,
    places_ref,
    charges_ref,
    hartley_ref,
    depth_ref,
    back_ref,
    values_ref,
    terms_ref,
    atom_planes,
    atom_columns,
    mesh,
):
    groups, cells, unused, atoms = places_ref.shape
    lanes = 2 * M

    def spread_group(group, carry):
        for cell in range(cells):
            places = places_ref[group, cell]
            fractions = spline_weights(places[3:6])
            bases = places[0:3].astype(jnp.int32)
            window = lax.broadcasted_iota(jnp.int32, (8, atoms), 0)
            along_depth = pick_weight(
                window - (bases[0:1] - group * planes), [w[0:1] for w in fractions]
            )
            index = lax.broadcasted_iota(jnp.int32, (M, atoms), 0)
            along_rows = pick_weight((index - bases[1:2]) & (M - 1), [w[1:2] for w in fractions])
            along_columns = pick_weight(
                (index - bases[2:3]) & (M - 1), [w[2:3] for w in fractions]
            )
            both = jnp.concatenate(
                [stacked_parts(along_rows), stacked_parts(along_columns)], axis=1
            )
            waves = jnp.dot(hartley_ref[...], both, preferred_element_type=jnp.float32)
            row_waves = waves[:, :atoms]
            column_waves = waves[:, atoms:]
            plane_waves = (
                (row_waves[:, None, :] * along_depth[None, :, :])
                .reshape(M * 8, atoms)
                .astype(jnp.bfloat16)
            )
            charges = charges_ref[group, cell]
            terms = jnp.concatenate(
                [column_waves * charges[0:1], column_waves * charges[1:2]], axis=0
            ).astype(jnp.bfloat16)
            atom_planes[group, cell] = plane_waves
            atom_columns[group, cell] = column_waves
            added = lax.dot_general(
                plane_waves, terms, (((1,), (1,)), ((), ())), preferred_element_type=jnp.float32
            )
            mesh[:, pl.ds(pl.multiple_of(group * 8, 8), 8), cell * lanes : (cell + 1) * lanes] = (
                added.reshape(M, 8, lanes)
            )
        return carry

    lax.fori_loop(0, groups, spread_group, 0)

    amplitude = params_ref[0]
    widths = params_ref[1]
    screens = params_ref[2]
    plane_squares = wave_squares(
        lax.broadcasted_iota(jnp.int32, (M, lanes), 0)
    ) + wave_squares(lax.broadcasted_iota(jnp.int32, (M, lanes), 1) & (M - 1))

    def filter_row(row, sums):
        spectrum = jnp.dot(
            depth_ref[...], stacked_parts(mesh[row]), preferred_element_type=jnp.float32
        )
        signed = jnp.where(row < M // 2, row, row - M).astype(jnp.float32)
        squares = plane_squares + signed * signed * ((2.0 * math.pi / M) ** 2)
        screened = 1.0 / (squares + screens)
        gains = (amplitude * (1.0 / M**3)) * jnp.exp((-0.5 * widths) * squares) * screened
        crossed = jnp.zeros((M, lanes), jnp.float32)
        filtered = []
        for cell in range(cells):
            part = spectrum[:, cell * lanes : (cell + 1) * lanes]
            crossed = crossed + part * pltpu.roll(part, M, 1)
            filtered.append(part * gains)
        crossed = crossed * gains
        mesh[row] = jnp.dot(
            back_ref[...],
            stacked_parts(jnp.concatenate(filtered, axis=1)),
            preferred_element_type=jnp.float32,
        )
        pieces = (crossed, crossed * squares, crossed * screened)
        return tuple(
            total + jnp.sum(piece.reshape(M // 8, 8, lanes), axis=0)
            for total, piece in zip(sums, pieces)
        )

    zero = jnp.zeros((8, lanes), jnp.float32)
    sums = lax.fori_loop(0, M, filter_row, (zero, zero, zero))
    for order_index in range(3):
        terms_ref[order_index] = sums[order_index]

    def read_group(group, carry):
        for cell in range(cells):
            window = (
                mesh[
                    :, pl.ds(pl.multiple_of(group * 8, 8), 8), cell * lanes : (cell + 1) * lanes
                ]
                .reshape(M * 8, lanes)
                .astype(jnp.bfloat16)
            )
            inner = lax.dot_general(
                window,
                atom_planes[group, cell],
                (((0,), (0,)), ((), ())),
                preferred_element_type=jnp.float32,
            )
            weighted = inner.reshape(2, M, atoms) * atom_columns[group, cell][None]
            values_ref[group, cell] = jnp.sum(weighted, axis=1)
        return carry

    lax.fori_loop(0, groups, read_group, 0)


def mesh_of_channel(params, places, charges):
    groups, cells, unused, atoms = places.shape
    planes = M // groups
    tables = stacked_tables(planes)
    whole = pl.BlockSpec(memory_space=pltpu.VMEM)
    return pl.pallas_call(
        functools.partial(mesh_kernel, planes),
        out_shape=(
            jax.ShapeDtypeStruct((groups, cells, 2, atoms), jnp.float32),
            jax.ShapeDtypeStruct((3, 8, 2 * M), jnp.float32),
        ),
        in_specs=[pl.BlockSpec(memory_space=pltpu.SMEM)] + [whole] * 5,
        out_specs=(whole, whole),
        scratch_shapes=[
            pltpu.VMEM((groups, cells, M * 8, atoms), jnp.bfloat16),
            pltpu.VMEM((groups, cells, M, atoms), jnp.float32),
            pltpu.VMEM((M, groups * 8, cells * 2 * M), jnp.float32),
        ],
        compiler_params=pltpu.CompilerParams(vmem_limit_bytes=56 * 1024 * 1024),
    )(params, places, charges, *tables)


def by_channel(
    atom_features,
    cotangent,
    charge_weight,
    message_weight,
    amplitude,
    smoothing,
    screening,
    base_cells,
    cell_offsets,
    row_starts,
    block_counts,
):
    cell_count, atom_rows, features = atom_features.shape
    channels = charge_weight.shape[1]
    devices = lax.axis_size("seq")
    blocks = block_counts.shape[1]
    channel = lax.axis_index("seq")
    places = lax.all_gather(
        jnp.concatenate([base_cells.astype(jnp.float32), cell_offsets], axis=1), "seq"
    )
    slot_index = jnp.arange(atom_rows // blocks, dtype=jnp.int32)
    live = (slot_index[None, None, :] < block_counts[:, :, None]).reshape(cell_count, atom_rows)
    live_mask = live.astype(jnp.float32)
    projected = lax.dot_general(
        charge_weight,
        atom_features,
        (((0,), (2,)), ((), ())),
        preferred_element_type=jnp.float32,
    )
    pulled = lax.dot_general(
        message_weight, cotangent, (((1,), (2,)), ((), ())), preferred_element_type=jnp.float32
    )
    charges = (jnp.stack([projected, pulled], axis=2) * live_mask[None, :, None, :]).astype(
        jnp.bfloat16
    )
    own_charges = lax.all_to_all(charges, "seq", split_axis=0, concat_axis=0, tiled=True)
    params = lax.dynamic_slice_in_dim(
        jnp.stack([amplitude, smoothing * smoothing, screening * screening]), channel, 1, 1
    ).reshape(3)
    values, sums = mesh_of_channel(params, places, own_charges.astype(jnp.float32))
    returned = lax.all_to_all(
        values.astype(jnp.bfloat16), "seq", split_axis=0, concat_axis=0, tiled=True
    )
    potential = returned[:, :, 0]
    response = jnp.where(live[None], returned[:, :, 1], jnp.zeros((), jnp.bfloat16))
    outgoing = lax.dot_general(
        potential, message_weight, (((0,), (0,)), ((), ())), preferred_element_type=jnp.float32
    )
    message = (live_mask[:, :, None] * outgoing).astype(jnp.bfloat16)
    atom_gradient = lax.dot_general(
        response, charge_weight, (((0,), (1,)), ((), ())), preferred_element_type=jnp.float32
    ).astype(jnp.bfloat16)
    gradient_scale = 1.0 / math.sqrt(cell_count * atom_rows * devices)
    live_potential = jnp.where(live[None], potential, jnp.zeros((), jnp.bfloat16))
    gradient_in = (
        lax.dot_general(
            atom_features,
            response,
            (((0, 1), (1, 2)), ((), ())),
            preferred_element_type=jnp.float32,
        )
        * gradient_scale
    )
    gradient_out = (
        lax.dot_general(
            live_potential,
            cotangent,
            (((1, 2), (0, 1)), ((), ())),
            preferred_element_type=jnp.float32,
        )
        * gradient_scale
    )
    factors = jnp.stack([jnp.ones((), jnp.float32), -params[1], -2.0 * params[2]])
    own_terms = jnp.sum(sums, axis=(1, 2)) * factors * (0.5 * gradient_scale)
    filter_terms = jnp.where(
        jnp.arange(channels)[None, :] == channel, own_terms[:, None], jnp.zeros((), jnp.float32)
    )
    gradient_in, gradient_out, filter_terms = lax.psum(
        (gradient_in, gradient_out, filter_terms), "seq"
    )
    return (message, atom_gradient, gradient_in, gradient_out, filter_terms)


def solution(mesh):

    def per_device(*arguments):
        by_channels = arguments[2].shape[1] == mesh.shape["seq"]
        return (by_channel if by_channels else on_device)(*arguments)

    in_specs = (
        P("groups", "seq", None),
        P("groups", "seq", None),
        P(),
        P(),
        P(),
        P(),
        P(),
        P("groups", None, "seq"),
        P("groups", None, "seq"),
        P("groups", "seq"),
        P("groups", "seq"),
    )
    out_specs = (
        P("groups", "seq", None),
        P("groups", "seq", None),
        P("groups", None),
        P("groups", None),
        P("groups", None),
    )
    return jax.shard_map(
        per_device, mesh=mesh, in_specs=in_specs, out_specs=out_specs, check_vma=False
    )
```

```python
import functools
import math

import jax
import jax.numpy as jnp
import ml_dtypes
import numpy as np
from jax import lax
from jax.experimental import pallas as pl
from jax.experimental.pallas import tpu as pltpu
from jax.sharding import PartitionSpec as P

M = 64
BAND = 32


def passed_along(value, axis, by):
    count = lax.axis_size(axis)
    return lax.ppermute(value, axis, [(i, (i + by) % count) for i in range(count)])


def spline_weights(fraction):
    remain = 1.0 - fraction
    square = fraction * fraction
    cubed = square * fraction
    return (
        remain * remain * remain / 6.0,
        (3.0 * cubed - 6.0 * square + 4.0) / 6.0,
        (-3.0 * cubed + 3.0 * square + 3.0 * fraction + 1.0) / 6.0,
        cubed / 6.0,
    )


def pick_weight(lattice_gap, weights):
    picked = jnp.where(lattice_gap == 0, weights[0], 0.0)
    for order_index in range(1, 4):
        picked = picked + jnp.where(lattice_gap == order_index, weights[order_index], 0.0)
    return picked


def atom_weights(base_cells, cell_offsets, row_start, plane_start, plane_count):
    atom_count = base_cells.shape[1]
    depth_index = plane_start + jnp.arange(plane_count, dtype=jnp.int32)
    row_index = row_start + jnp.arange(BAND, dtype=jnp.int32)
    column_index = jnp.arange(M, dtype=jnp.int32)
    along_depth = pick_weight(
        (depth_index[None, :] - base_cells[0][:, None]) % M,
        spline_weights(cell_offsets[0][:, None]),
    )
    along_rows = pick_weight(
        (row_index[None, :] - base_cells[1][:, None]) % M, spline_weights(cell_offsets[1][:, None])
    )
    along_columns = pick_weight(
        (column_index[None, :] - base_cells[2][:, None]) % M,
        spline_weights(cell_offsets[2][:, None]),
    )
    plane_rows = (
        (along_depth[:, :, None] * along_rows[:, None, :])
        .reshape(atom_count, plane_count * BAND)
        .astype(jnp.bfloat16)
    )
    return (plane_rows, along_columns)


def hartley_table():
    indices = jnp.arange(M, dtype=jnp.int32)
    product = indices[:, None] * indices[None, :] % M
    angles = product.astype(jnp.float32) * (2.0 * math.pi / M)
    return jnp.cos(angles) + jnp.sin(angles)


def wave_numbers(indices):
    return jnp.where(indices < M // 2, indices, indices - M).astype(jnp.float32) * (
        2.0 * math.pi / M
    )


def squared_waves(row_first, row_count):
    depth_waves = wave_numbers(jnp.arange(M, dtype=jnp.int32))
    row_waves = wave_numbers(row_first + jnp.arange(row_count, dtype=jnp.int32))
    summed = (
        depth_waves[:, None, None] ** 2
        + row_waves[None, :, None] ** 2
        + depth_waves[None, None, :] ** 2
    )
    return summed[:, :, None, :]


def scaled_filter(amplitude, smoothing, screening, wave_square):
    gains = amplitude[None, None, :, None]
    widths = (smoothing * smoothing)[None, None, :, None]
    screens = (screening * screening)[None, None, :, None]
    return gains * jnp.exp(-0.5 * widths * wave_square) / (wave_square + screens) * (1.0 / M**3)


def spread_cell(charges, base_cells, cell_offsets, row_starts, plane_start, plane_count):
    blocks = row_starts.shape[0]
    atom_count = charges.shape[0] // blocks
    columns = charges.shape[1] * M

    def add_block(padded, block_index):
        first_row = block_index * atom_count
        block_charges = lax.dynamic_slice_in_dim(charges, first_row, atom_count, 0)
        block_cells = lax.dynamic_slice_in_dim(base_cells, first_row, atom_count, 1)
        block_offsets = lax.dynamic_slice_in_dim(cell_offsets, first_row, atom_count, 1)
        row_start = row_starts[block_index]
        plane_rows, along_columns = atom_weights(
            block_cells, block_offsets, row_start, plane_start, plane_count
        )
        spread_rows = (
            (block_charges.astype(jnp.float32)[:, :, None] * along_columns[:, None, :])
            .reshape(atom_count, columns)
            .astype(jnp.bfloat16)
        )
        addition = lax.dot_general(
            plane_rows, spread_rows, (((0,), (0,)), ((), ())), preferred_element_type=jnp.float32
        )
        addition = addition.reshape(plane_count, BAND, columns)
        current = lax.dynamic_slice_in_dim(padded, row_start, BAND, 1)
        return (lax.dynamic_update_slice_in_dim(padded, current + addition, row_start, 1), None)

    padded = jnp.zeros((plane_count, M + BAND, columns), jnp.float32)
    padded, unused = lax.scan(add_block, padded, jnp.arange(blocks, dtype=jnp.int32))
    return padded[:, :M].at[:, :BAND].add(padded[:, M:])


def interpolate_cell(mesh, base_cells, cell_offsets, row_starts, plane_start):
    plane_count = mesh.shape[0]
    blocks = row_starts.shape[0]
    atom_count = base_cells.shape[1] // blocks
    padded = jnp.concatenate([mesh, mesh[:, :BAND]], axis=1)

    def one_block(block_index):
        first_row = block_index * atom_count
        block_cells = lax.dynamic_slice_in_dim(base_cells, first_row, atom_count, 1)
        block_offsets = lax.dynamic_slice_in_dim(cell_offsets, first_row, atom_count, 1)
        row_start = row_starts[block_index]
        plane_rows, along_columns = atom_weights(
            block_cells, block_offsets, row_start, plane_start, plane_count
        )
        window = lax.dynamic_slice_in_dim(padded, row_start, BAND, 1).reshape(
            plane_count * BAND, -1
        )
        values = jnp.dot(plane_rows, window, preferred_element_type=jnp.float32)
        return jnp.sum(values.reshape(atom_count, -1, M) * along_columns[:, None, :], axis=2)

    return lax.map(one_block, jnp.arange(blocks, dtype=jnp.int32)).reshape(blocks * atom_count, -1)


def spread_cells(charges, base_cells, cell_offsets, row_starts, plane_start, plane_count):

    def spread_one_cell(cell_data):
        return spread_cell(
            cell_data[0], cell_data[1], cell_data[2], cell_data[3], plane_start, plane_count
        )

    return lax.map(spread_one_cell, (charges, base_cells, cell_offsets, row_starts))


def interpolate_cells(mesh, base_cells, cell_offsets, row_starts, plane_start):

    def interpolate_one_cell(cell_data):
        return interpolate_cell(cell_data[0], cell_data[1], cell_data[2], cell_data[3], plane_start)

    return lax.map(interpolate_one_cell, (mesh, base_cells, cell_offsets, row_starts))


def long_range(charges, base_cells, cell_offsets, row_starts, spectral_filter):
    devices = lax.axis_size("seq")
    planes = M // devices
    spill_reach = (planes + 2) // planes
    plane_start = lax.axis_index("seq") * planes
    cell_count = charges.shape[0]
    channels = charges.shape[2]
    hartley = hartley_table()
    highest = lax.Precision.HIGHEST
    extended = spread_cells(charges, base_cells, cell_offsets, row_starts, plane_start, planes + 3)
    mesh_field = extended[:, :planes]
    for distance in range(1, spill_reach + 1):
        lower_plane = (distance - 1) * planes
        upper_plane = min(distance * planes, 3)
        arrived = passed_along(
            extended[:, planes + lower_plane : planes + upper_plane], "seq", distance
        )
        mesh_field = mesh_field.at[:, : upper_plane - lower_plane].add(arrived)
    slab_data = mesh_field.reshape(cell_count, planes, M, channels, M)
    spectrum = jnp.einsum("kpycx,xf->kpycf", slab_data, hartley, precision=highest)
    spectrum = jnp.einsum("kpycx,yf->kpfcx", spectrum, hartley, precision=highest)
    forward = jnp.einsum(
        "kzycx,zf->kfycx",
        lax.all_to_all(spectrum, "seq", split_axis=2, concat_axis=1, tiled=True),
        hartley,
        precision=highest,
    )
    weighted = spectral_filter[None] * forward
    returned = jnp.einsum("kzycx,zf->kfycx", weighted, hartley, precision=highest)
    slab_back = lax.all_to_all(returned, "seq", split_axis=1, concat_axis=2, tiled=True)
    slab_back = jnp.einsum("kpycx,yf->kpfcx", slab_back, hartley, precision=highest)
    slab_back = jnp.einsum("kpycx,xf->kpycf", slab_back, hartley, precision=highest)
    rounded = slab_back.reshape(cell_count, planes, M, channels * M).astype(jnp.bfloat16)
    pieces = [rounded]
    for distance in range(1, spill_reach + 1):
        lower_plane = (distance - 1) * planes
        upper_plane = min(distance * planes, 3)
        pieces.append(passed_along(rounded[:, : upper_plane - lower_plane], "seq", -distance))
    values = interpolate_cells(
        jnp.concatenate(pieces, axis=1), base_cells, cell_offsets, row_starts, plane_start
    )
    return (values, forward)


def on_device(
    atom_features,
    cotangent,
    charge_weight,
    message_weight,
    amplitude,
    smoothing,
    screening,
    base_cells,
    cell_offsets,
    row_starts,
    block_counts,
):
    cell_count, atom_rows, features = atom_features.shape
    channels = charge_weight.shape[1]
    devices = lax.axis_size("seq")
    blocks = block_counts.shape[1]
    slot_index = jnp.arange(atom_rows // blocks, dtype=jnp.int32)
    live_mask = (
        (slot_index[None, None, :] < block_counts[:, :, None])
        .reshape(cell_count, atom_rows)
        .astype(jnp.float32)
    )
    projected = jnp.dot(
        atom_features.reshape(-1, features), charge_weight, preferred_element_type=jnp.float32
    )
    charges = (live_mask[:, :, None] * projected.reshape(cell_count, atom_rows, channels)).astype(
        jnp.bfloat16
    )
    pulled = lax.dot_general(
        cotangent.reshape(-1, features),
        message_weight,
        (((1,), (1,)), ((), ())),
        preferred_element_type=jnp.float32,
    )
    adjoint = (live_mask[:, :, None] * pulled.reshape(cell_count, atom_rows, channels)).astype(
        jnp.bfloat16
    )
    row_count = M // devices
    wave_square = squared_waves(lax.axis_index("seq") * row_count, row_count)
    spectral_filter = scaled_filter(amplitude, smoothing, screening, wave_square)
    potential, source_spectra = long_range(
        charges, base_cells, cell_offsets, row_starts, spectral_filter
    )
    response, adjoint_spectra = long_range(
        adjoint, base_cells, cell_offsets, row_starts, spectral_filter
    )
    potential_rounded = potential.astype(jnp.bfloat16)
    outgoing = jnp.dot(
        potential_rounded.reshape(-1, channels), message_weight, preferred_element_type=jnp.float32
    )
    message = (live_mask[:, :, None] * outgoing.reshape(cell_count, atom_rows, features)).astype(
        jnp.bfloat16
    )
    response_rounded = (live_mask[:, :, None] * response).astype(jnp.bfloat16)
    backward = lax.dot_general(
        response_rounded.reshape(-1, channels),
        charge_weight,
        (((1,), (1,)), ((), ())),
        preferred_element_type=jnp.float32,
    )
    atom_gradient = backward.reshape(cell_count, atom_rows, features).astype(jnp.bfloat16)
    gradient_scale = 1.0 / math.sqrt(cell_count * atom_rows * devices)
    masked_cotangent = jnp.where(live_mask[:, :, None] > 0, cotangent, jnp.zeros((), jnp.bfloat16))
    gradient_in = (
        lax.dot_general(
            atom_features.reshape(-1, features),
            response_rounded.reshape(-1, channels),
            (((0,), (0,)), ((), ())),
            preferred_element_type=jnp.float32,
        )
        * gradient_scale
    )
    gradient_out = (
        lax.dot_general(
            potential_rounded.reshape(-1, channels),
            masked_cotangent.reshape(-1, features),
            (((0,), (0,)), ((), ())),
            preferred_element_type=jnp.float32,
        )
        * gradient_scale
    )
    intersection = jnp.sum(source_spectra * adjoint_spectra, axis=0) * spectral_filter
    widths = (smoothing * smoothing)[None, None, :, None]
    screens = (screening * screening)[None, None, :, None]
    smooth_factor = -widths * wave_square
    screen_factor = -2.0 * screens / (wave_square + screens)
    filter_terms = (
        jnp.stack(
            [
                jnp.sum(intersection, axis=(0, 1, 3)),
                jnp.sum(intersection * smooth_factor, axis=(0, 1, 3)),
                jnp.sum(intersection * screen_factor, axis=(0, 1, 3)),
            ]
        )
        * gradient_scale
    )
    gradient_in, gradient_out, filter_terms = lax.psum(
        (gradient_in, gradient_out, filter_terms), "seq"
    )
    return (message, atom_gradient, gradient_in, gradient_out, filter_terms)


def stacked_tables(planes):
    indices = np.arange(M)
    angles = (indices[:, None] * indices[None, :] % M) * (2.0 * np.pi / M)
    hartley = (np.cos(angles) + np.sin(angles)).astype(np.float32)
    window = (np.arange(M // planes)[:, None] * planes + np.arange(8)[None, :]) % M
    depth = hartley[:, window.reshape(-1)]

    def parts(table):
        high = table.astype(ml_dtypes.bfloat16)
        low = (table - high.astype(np.float32)).astype(ml_dtypes.bfloat16)
        return jnp.asarray(np.concatenate([high, high, low], axis=1))

    return (parts(hartley), parts(depth), parts(depth.T))


def stacked_parts(value):
    high = value.astype(jnp.bfloat16)
    low = (value - high.astype(jnp.float32)).astype(jnp.bfloat16)
    return jnp.concatenate([high, low, high], axis=0)


def wave_squares(indices):
    waves = jnp.where(indices < M // 2, indices, indices - M).astype(jnp.float32)
    return waves * waves * ((2.0 * math.pi / M) ** 2)


def mesh_kernel(
    planes,
    params_ref,
    atoms_ref,
    hartley_ref,
    depth_ref,
    back_ref,
    values_ref,
    terms_ref,
    atom_planes,
    atom_columns,
    mesh,
):
    groups, cells, unused, atoms = atoms_ref.shape
    lanes = 2 * M

    def spread_group(group, carry):
        for cell in range(cells):
            places = atoms_ref[group, cell]
            fractions = spline_weights(places[3:6])
            bases = places[0:3].astype(jnp.int32)
            window = lax.broadcasted_iota(jnp.int32, (8, atoms), 0)
            along_depth = pick_weight(
                window - (bases[0:1] - group * planes), [w[0:1] for w in fractions]
            )
            index = lax.broadcasted_iota(jnp.int32, (M, atoms), 0)
            along_rows = pick_weight((index - bases[1:2]) & (M - 1), [w[1:2] for w in fractions])
            along_columns = pick_weight(
                (index - bases[2:3]) & (M - 1), [w[2:3] for w in fractions]
            )
            both = jnp.concatenate(
                [stacked_parts(along_rows), stacked_parts(along_columns)], axis=1
            )
            waves = jnp.dot(hartley_ref[...], both, preferred_element_type=jnp.float32)
            row_waves = waves[:, :atoms]
            column_waves = waves[:, atoms:]
            plane_waves = (
                (row_waves[:, None, :] * along_depth[None, :, :])
                .reshape(M * 8, atoms)
                .astype(jnp.bfloat16)
            )
            terms = jnp.concatenate(
                [column_waves * places[6:7], column_waves * places[7:8]], axis=0
            ).astype(jnp.bfloat16)
            atom_planes[group, cell] = plane_waves
            atom_columns[group, cell] = column_waves
            added = lax.dot_general(
                plane_waves, terms, (((1,), (1,)), ((), ())), preferred_element_type=jnp.float32
            )
            mesh[:, pl.ds(pl.multiple_of(group * 8, 8), 8), cell * lanes : (cell + 1) * lanes] = (
                added.reshape(M, 8, lanes)
            )
        return carry

    lax.fori_loop(0, groups, spread_group, 0)

    amplitude = params_ref[0]
    widths = params_ref[1]
    screens = params_ref[2]
    plane_squares = wave_squares(
        lax.broadcasted_iota(jnp.int32, (M, lanes), 0)
    ) + wave_squares(lax.broadcasted_iota(jnp.int32, (M, lanes), 1) & (M - 1))

    def filter_row(row, sums):
        spectrum = jnp.dot(
            depth_ref[...], stacked_parts(mesh[row]), preferred_element_type=jnp.float32
        )
        signed = jnp.where(row < M // 2, row, row - M).astype(jnp.float32)
        squares = plane_squares + signed * signed * ((2.0 * math.pi / M) ** 2)
        screened = 1.0 / (squares + screens)
        gains = (amplitude * (1.0 / M**3)) * jnp.exp((-0.5 * widths) * squares) * screened
        crossed = jnp.zeros((M, lanes), jnp.float32)
        filtered = []
        for cell in range(cells):
            part = spectrum[:, cell * lanes : (cell + 1) * lanes]
            crossed = crossed + part * pltpu.roll(part, M, 1)
            filtered.append(part * gains)
        crossed = crossed * gains
        mesh[row] = jnp.dot(
            back_ref[...],
            stacked_parts(jnp.concatenate(filtered, axis=1)),
            preferred_element_type=jnp.float32,
        )
        pieces = (crossed, crossed * squares, crossed * screened)
        return tuple(
            total + jnp.sum(piece.reshape(M // 8, 8, lanes), axis=0)
            for total, piece in zip(sums, pieces)
        )

    zero = jnp.zeros((8, lanes), jnp.float32)
    sums = lax.fori_loop(0, M, filter_row, (zero, zero, zero))
    for order_index in range(3):
        terms_ref[order_index] = sums[order_index]

    def read_group(group, carry):
        for cell in range(cells):
            window = (
                mesh[
                    :, pl.ds(pl.multiple_of(group * 8, 8), 8), cell * lanes : (cell + 1) * lanes
                ]
                .reshape(M * 8, lanes)
                .astype(jnp.bfloat16)
            )
            inner = lax.dot_general(
                window,
                atom_planes[group, cell],
                (((0,), (0,)), ((), ())),
                preferred_element_type=jnp.float32,
            )
            weighted = inner.reshape(2, M, atoms) * atom_columns[group, cell][None]
            values_ref[group, cell] = jnp.sum(weighted, axis=1)
        return carry

    lax.fori_loop(0, groups, read_group, 0)


def mesh_of_channel(params, atom_blocks):
    groups, cells, unused, atoms = atom_blocks.shape
    planes = M // groups
    tables = stacked_tables(planes)
    whole = pl.BlockSpec(memory_space=pltpu.VMEM)
    return pl.pallas_call(
        functools.partial(mesh_kernel, planes),
        out_shape=(
            jax.ShapeDtypeStruct((groups, cells, 2, atoms), jnp.float32),
            jax.ShapeDtypeStruct((3, 8, 2 * M), jnp.float32),
        ),
        in_specs=[pl.BlockSpec(memory_space=pltpu.SMEM)] + [whole] * 4,
        out_specs=(whole, whole),
        scratch_shapes=[
            pltpu.VMEM((groups, cells, M * 8, atoms), jnp.bfloat16),
            pltpu.VMEM((groups, cells, M, atoms), jnp.float32),
            pltpu.VMEM((M, groups * 8, cells * 2 * M), jnp.float32),
        ],
        compiler_params=pltpu.CompilerParams(vmem_limit_bytes=56 * 1024 * 1024),
    )(params, atom_blocks, *tables)


def to_peer(source, target, send_sems, receive_sems, peer, sender):
    return pltpu.make_async_remote_copy(
        src_ref=source,
        dst_ref=target,
        send_sem=send_sems.at[peer],
        recv_sem=receive_sems.at[sender],
        device_id={"seq": peer},
        device_id_type=pl.DeviceIdType.MESH,
    )


def greet_peers(count, own):
    barrier = pltpu.get_barrier_semaphore()

    def greet(step, carry):
        pl.semaphore_signal(
            barrier,
            inc=1,
            device_id={"seq": lax.rem(own + step, count)},
            device_id_type=pl.DeviceIdType.MESH,
        )
        return carry

    lax.fori_loop(1, count, greet, 0)
    pl.semaphore_wait(barrier, count - 1)


def exchange_kernel(count, given_ref, taken_ref, send_sems, receive_sems):
    own = lax.axis_index("seq")
    greet_peers(count, own)

    def send(step, carry):
        peer = lax.rem(own + step, count)
        to_peer(
            given_ref.at[peer], taken_ref.at[own], send_sems, receive_sems, peer, own
        ).start()
        return carry

    lax.fori_loop(1, count, send, 0)
    taken_ref[own] = given_ref[own]

    def finish(step, carry):
        peer = lax.rem(own + step, count)
        copy = to_peer(
            given_ref.at[peer], taken_ref.at[peer], send_sems, receive_sems, peer, peer
        )
        copy.wait_send()
        copy.wait_recv()
        return carry

    lax.fori_loop(1, count, finish, 0)


def exchanged(blocks, collective_id):
    count = blocks.shape[0]
    whole = pl.BlockSpec(memory_space=pltpu.VMEM)
    return pl.pallas_call(
        functools.partial(exchange_kernel, count),
        out_shape=jax.ShapeDtypeStruct(blocks.shape, blocks.dtype),
        in_specs=[whole],
        out_specs=whole,
        scratch_shapes=[
            pltpu.SemaphoreType.DMA((count,)),
            pltpu.SemaphoreType.DMA((count,)),
        ],
        compiler_params=pltpu.CompilerParams(collective_id=collective_id, has_side_effects=True),
    )(blocks)


def total_kernel(
    count, given_ref, fixed_ref, totals_ref, landed, send_sems, receive_sems, spread_sems, total_sems
):
    own = lax.axis_index("seq")
    greet_peers(count, own)

    def send(step, carry):
        peer = lax.rem(own + step, count)
        to_peer(given_ref.at[peer], landed.at[own], send_sems, receive_sems, peer, own).start()
        return carry

    lax.fori_loop(1, count, send, 0)

    def gather(step, total):
        peer = lax.rem(own + step, count)
        copy = to_peer(given_ref.at[peer], landed.at[peer], send_sems, receive_sems, peer, peer)
        copy.wait_send()
        copy.wait_recv()
        return total + landed[peer]

    totals_ref[own] = lax.fori_loop(1, count, gather, given_ref[own] + fixed_ref[...])

    def spread(step, carry):
        peer = lax.rem(own + step, count)
        to_peer(totals_ref.at[own], totals_ref.at[own], spread_sems, total_sems, peer, own).start()
        return carry

    lax.fori_loop(1, count, spread, 0)

    def finish(step, carry):
        peer = lax.rem(own + step, count)
        copy = to_peer(
            totals_ref.at[own], totals_ref.at[peer], spread_sems, total_sems, peer, peer
        )
        copy.wait_send()
        copy.wait_recv()
        return carry

    lax.fori_loop(1, count, finish, 0)


def totals_of_channels(blocks, fixed, collective_id):
    count = blocks.shape[0]
    whole = pl.BlockSpec(memory_space=pltpu.VMEM)
    sems = pltpu.SemaphoreType.DMA((count,))
    return pl.pallas_call(
        functools.partial(total_kernel, count),
        out_shape=jax.ShapeDtypeStruct(blocks.shape, blocks.dtype),
        in_specs=[whole, whole],
        out_specs=whole,
        scratch_shapes=[pltpu.VMEM(blocks.shape, blocks.dtype), sems, sems, sems, sems],
        compiler_params=pltpu.CompilerParams(collective_id=collective_id, has_side_effects=True),
    )(blocks, fixed)


def by_channel(
    atom_features,
    cotangent,
    charge_weight,
    message_weight,
    amplitude,
    smoothing,
    screening,
    base_cells,
    cell_offsets,
    row_starts,
    block_counts,
):
    cell_count, atom_rows, features = atom_features.shape
    channels = charge_weight.shape[1]
    devices = lax.axis_size("seq")
    blocks = block_counts.shape[1]
    channel = lax.axis_index("seq")
    slot_index = jnp.arange(atom_rows // blocks, dtype=jnp.int32)
    live = (slot_index[None, None, :] < block_counts[:, :, None]).reshape(cell_count, atom_rows)
    live_mask = live.astype(jnp.float32)
    projected = lax.dot_general(
        charge_weight,
        atom_features,
        (((0,), (2,)), ((), ())),
        preferred_element_type=jnp.float32,
    )
    pulled = lax.dot_general(
        message_weight, cotangent, (((1,), (2,)), ((), ())), preferred_element_type=jnp.float32
    )
    charges = (jnp.stack([projected, pulled], axis=2) * live_mask[None, :, None, :]).astype(
        jnp.bfloat16
    )
    places = jnp.concatenate([base_cells.astype(jnp.float32), cell_offsets], axis=1)
    blocks_out = jnp.concatenate(
        [
            jnp.broadcast_to(places[None], (devices,) + places.shape),
            charges.astype(jnp.float32),
        ],
        axis=2,
    )
    atoms_in = exchanged(blocks_out, 0)
    params = lax.dynamic_slice_in_dim(
        jnp.stack([amplitude, smoothing * smoothing, screening * screening]), channel, 1, 1
    ).reshape(3)
    values, sums = mesh_of_channel(params, atoms_in)
    returned = exchanged(values, 1).astype(jnp.bfloat16)
    potential = returned[:, :, 0]
    response = jnp.where(live[None], returned[:, :, 1], jnp.zeros((), jnp.bfloat16))
    outgoing = lax.dot_general(
        potential, message_weight, (((0,), (0,)), ((), ())), preferred_element_type=jnp.float32
    )
    message = (live_mask[:, :, None] * outgoing).astype(jnp.bfloat16)
    atom_gradient = lax.dot_general(
        response, charge_weight, (((0,), (1,)), ((), ())), preferred_element_type=jnp.float32
    ).astype(jnp.bfloat16)
    gradient_scale = 1.0 / math.sqrt(cell_count * atom_rows * devices)
    live_potential = jnp.where(live[None], potential, jnp.zeros((), jnp.bfloat16))
    gradient_in = lax.dot_general(
        response,
        atom_features,
        (((1, 2), (0, 1)), ((), ())),
        preferred_element_type=jnp.float32,
    )
    gradient_out = lax.dot_general(
        live_potential,
        cotangent,
        (((1, 2), (0, 1)), ((), ())),
        preferred_element_type=jnp.float32,
    )
    factors = jnp.stack([jnp.ones((), jnp.float32), -params[1], -2.0 * params[2]])
    own_terms = jnp.sum(sums, axis=(1, 2)) * factors * 0.5
    width = 128
    rows = features // width
    padding = 8 - 2 * rows
    blocks_out = jnp.concatenate(
        [
            gradient_in.reshape(channels, rows, width),
            gradient_out.reshape(channels, rows, width),
            jnp.zeros((channels, padding, width), jnp.float32),
        ],
        axis=1,
    )
    fixed = jnp.pad(own_terms[None, :], ((2 * rows, padding - 1), (0, width - 3)))
    totals = totals_of_channels(blocks_out, fixed, 2) * gradient_scale
    gradient_in = totals[:, :rows].reshape(channels, features).T
    gradient_out = totals[:, rows : 2 * rows].reshape(channels, features)
    filter_terms = totals[:, 2 * rows, :3].T
    return (message, atom_gradient, gradient_in, gradient_out, filter_terms)


def solution(mesh):

    def per_device(*arguments):
        by_channels = arguments[2].shape[1] == mesh.shape["seq"]
        return (by_channel if by_channels else on_device)(*arguments)

    in_specs = (
        P("groups", "seq", None),
        P("groups", "seq", None),
        P(),
        P(),
        P(),
        P(),
        P(),
        P("groups", None, "seq"),
        P("groups", None, "seq"),
        P("groups", "seq"),
        P("groups", "seq"),
    )
    out_specs = (
        P("groups", "seq", None),
        P("groups", "seq", None),
        P("groups", None),
        P("groups", None),
        P("groups", None),
    )
    return jax.shard_map(
        per_device, mesh=mesh, in_specs=in_specs, out_specs=out_specs, check_vma=False
    )
```

```python
import functools
import math

import jax
import jax.numpy as jnp
import ml_dtypes
import numpy as np
from jax import lax
from jax.experimental import pallas as pl
from jax.experimental.pallas import tpu as pltpu
from jax.sharding import PartitionSpec as P

M = 64
BAND = 32


def passed_along(value, axis, by):
    count = lax.axis_size(axis)
    return lax.ppermute(value, axis, [(i, (i + by) % count) for i in range(count)])


def spline_weights(fraction):
    remain = 1.0 - fraction
    square = fraction * fraction
    cubed = square * fraction
    return (
        remain * remain * remain / 6.0,
        (3.0 * cubed - 6.0 * square + 4.0) / 6.0,
        (-3.0 * cubed + 3.0 * square + 3.0 * fraction + 1.0) / 6.0,
        cubed / 6.0,
    )


def pick_weight(lattice_gap, weights):
    picked = jnp.where(lattice_gap == 0, weights[0], 0.0)
    for order_index in range(1, 4):
        picked = picked + jnp.where(lattice_gap == order_index, weights[order_index], 0.0)
    return picked


def atom_weights(base_cells, cell_offsets, row_start, plane_start, plane_count):
    atom_count = base_cells.shape[1]
    depth_index = plane_start + jnp.arange(plane_count, dtype=jnp.int32)
    row_index = row_start + jnp.arange(BAND, dtype=jnp.int32)
    column_index = jnp.arange(M, dtype=jnp.int32)
    along_depth = pick_weight(
        (depth_index[None, :] - base_cells[0][:, None]) % M,
        spline_weights(cell_offsets[0][:, None]),
    )
    along_rows = pick_weight(
        (row_index[None, :] - base_cells[1][:, None]) % M, spline_weights(cell_offsets[1][:, None])
    )
    along_columns = pick_weight(
        (column_index[None, :] - base_cells[2][:, None]) % M,
        spline_weights(cell_offsets[2][:, None]),
    )
    plane_rows = (
        (along_depth[:, :, None] * along_rows[:, None, :])
        .reshape(atom_count, plane_count * BAND)
        .astype(jnp.bfloat16)
    )
    return (plane_rows, along_columns)


def hartley_table():
    indices = jnp.arange(M, dtype=jnp.int32)
    product = indices[:, None] * indices[None, :] % M
    angles = product.astype(jnp.float32) * (2.0 * math.pi / M)
    return jnp.cos(angles) + jnp.sin(angles)


def wave_numbers(indices):
    return jnp.where(indices < M // 2, indices, indices - M).astype(jnp.float32) * (
        2.0 * math.pi / M
    )


def squared_waves(row_first, row_count):
    depth_waves = wave_numbers(jnp.arange(M, dtype=jnp.int32))
    row_waves = wave_numbers(row_first + jnp.arange(row_count, dtype=jnp.int32))
    summed = (
        depth_waves[:, None, None] ** 2
        + row_waves[None, :, None] ** 2
        + depth_waves[None, None, :] ** 2
    )
    return summed[:, :, None, :]


def scaled_filter(amplitude, smoothing, screening, wave_square):
    gains = amplitude[None, None, :, None]
    widths = (smoothing * smoothing)[None, None, :, None]
    screens = (screening * screening)[None, None, :, None]
    return gains * jnp.exp(-0.5 * widths * wave_square) / (wave_square + screens) * (1.0 / M**3)


def spread_cell(charges, base_cells, cell_offsets, row_starts, plane_start, plane_count):
    blocks = row_starts.shape[0]
    atom_count = charges.shape[0] // blocks
    columns = charges.shape[1] * M

    def add_block(padded, block_index):
        first_row = block_index * atom_count
        block_charges = lax.dynamic_slice_in_dim(charges, first_row, atom_count, 0)
        block_cells = lax.dynamic_slice_in_dim(base_cells, first_row, atom_count, 1)
        block_offsets = lax.dynamic_slice_in_dim(cell_offsets, first_row, atom_count, 1)
        row_start = row_starts[block_index]
        plane_rows, along_columns = atom_weights(
            block_cells, block_offsets, row_start, plane_start, plane_count
        )
        spread_rows = (
            (block_charges.astype(jnp.float32)[:, :, None] * along_columns[:, None, :])
            .reshape(atom_count, columns)
            .astype(jnp.bfloat16)
        )
        addition = lax.dot_general(
            plane_rows, spread_rows, (((0,), (0,)), ((), ())), preferred_element_type=jnp.float32
        )
        addition = addition.reshape(plane_count, BAND, columns)
        current = lax.dynamic_slice_in_dim(padded, row_start, BAND, 1)
        return (lax.dynamic_update_slice_in_dim(padded, current + addition, row_start, 1), None)

    padded = jnp.zeros((plane_count, M + BAND, columns), jnp.float32)
    padded, unused = lax.scan(add_block, padded, jnp.arange(blocks, dtype=jnp.int32))
    return padded[:, :M].at[:, :BAND].add(padded[:, M:])


def interpolate_cell(mesh, base_cells, cell_offsets, row_starts, plane_start):
    plane_count = mesh.shape[0]
    blocks = row_starts.shape[0]
    atom_count = base_cells.shape[1] // blocks
    padded = jnp.concatenate([mesh, mesh[:, :BAND]], axis=1)

    def one_block(block_index):
        first_row = block_index * atom_count
        block_cells = lax.dynamic_slice_in_dim(base_cells, first_row, atom_count, 1)
        block_offsets = lax.dynamic_slice_in_dim(cell_offsets, first_row, atom_count, 1)
        row_start = row_starts[block_index]
        plane_rows, along_columns = atom_weights(
            block_cells, block_offsets, row_start, plane_start, plane_count
        )
        window = lax.dynamic_slice_in_dim(padded, row_start, BAND, 1).reshape(
            plane_count * BAND, -1
        )
        values = jnp.dot(plane_rows, window, preferred_element_type=jnp.float32)
        return jnp.sum(values.reshape(atom_count, -1, M) * along_columns[:, None, :], axis=2)

    return lax.map(one_block, jnp.arange(blocks, dtype=jnp.int32)).reshape(blocks * atom_count, -1)


def spread_cells(charges, base_cells, cell_offsets, row_starts, plane_start, plane_count):

    def spread_one_cell(cell_data):
        return spread_cell(
            cell_data[0], cell_data[1], cell_data[2], cell_data[3], plane_start, plane_count
        )

    return lax.map(spread_one_cell, (charges, base_cells, cell_offsets, row_starts))


def interpolate_cells(mesh, base_cells, cell_offsets, row_starts, plane_start):

    def interpolate_one_cell(cell_data):
        return interpolate_cell(cell_data[0], cell_data[1], cell_data[2], cell_data[3], plane_start)

    return lax.map(interpolate_one_cell, (mesh, base_cells, cell_offsets, row_starts))


def long_range(charges, base_cells, cell_offsets, row_starts, spectral_filter):
    devices = lax.axis_size("seq")
    planes = M // devices
    spill_reach = (planes + 2) // planes
    plane_start = lax.axis_index("seq") * planes
    cell_count = charges.shape[0]
    channels = charges.shape[2]
    hartley = hartley_table()
    highest = lax.Precision.HIGHEST
    extended = spread_cells(charges, base_cells, cell_offsets, row_starts, plane_start, planes + 3)
    mesh_field = extended[:, :planes]
    for distance in range(1, spill_reach + 1):
        lower_plane = (distance - 1) * planes
        upper_plane = min(distance * planes, 3)
        arrived = passed_along(
            extended[:, planes + lower_plane : planes + upper_plane], "seq", distance
        )
        mesh_field = mesh_field.at[:, : upper_plane - lower_plane].add(arrived)
    slab_data = mesh_field.reshape(cell_count, planes, M, channels, M)
    spectrum = jnp.einsum("kpycx,xf->kpycf", slab_data, hartley, precision=highest)
    spectrum = jnp.einsum("kpycx,yf->kpfcx", spectrum, hartley, precision=highest)
    forward = jnp.einsum(
        "kzycx,zf->kfycx",
        lax.all_to_all(spectrum, "seq", split_axis=2, concat_axis=1, tiled=True),
        hartley,
        precision=highest,
    )
    weighted = spectral_filter[None] * forward
    returned = jnp.einsum("kzycx,zf->kfycx", weighted, hartley, precision=highest)
    slab_back = lax.all_to_all(returned, "seq", split_axis=1, concat_axis=2, tiled=True)
    slab_back = jnp.einsum("kpycx,yf->kpfcx", slab_back, hartley, precision=highest)
    slab_back = jnp.einsum("kpycx,xf->kpycf", slab_back, hartley, precision=highest)
    rounded = slab_back.reshape(cell_count, planes, M, channels * M).astype(jnp.bfloat16)
    pieces = [rounded]
    for distance in range(1, spill_reach + 1):
        lower_plane = (distance - 1) * planes
        upper_plane = min(distance * planes, 3)
        pieces.append(passed_along(rounded[:, : upper_plane - lower_plane], "seq", -distance))
    values = interpolate_cells(
        jnp.concatenate(pieces, axis=1), base_cells, cell_offsets, row_starts, plane_start
    )
    return (values, forward)


def on_device(
    atom_features,
    cotangent,
    charge_weight,
    message_weight,
    amplitude,
    smoothing,
    screening,
    base_cells,
    cell_offsets,
    row_starts,
    block_counts,
):
    cell_count, atom_rows, features = atom_features.shape
    channels = charge_weight.shape[1]
    devices = lax.axis_size("seq")
    blocks = block_counts.shape[1]
    slot_index = jnp.arange(atom_rows // blocks, dtype=jnp.int32)
    live_mask = (
        (slot_index[None, None, :] < block_counts[:, :, None])
        .reshape(cell_count, atom_rows)
        .astype(jnp.float32)
    )
    projected = jnp.dot(
        atom_features.reshape(-1, features), charge_weight, preferred_element_type=jnp.float32
    )
    charges = (live_mask[:, :, None] * projected.reshape(cell_count, atom_rows, channels)).astype(
        jnp.bfloat16
    )
    pulled = lax.dot_general(
        cotangent.reshape(-1, features),
        message_weight,
        (((1,), (1,)), ((), ())),
        preferred_element_type=jnp.float32,
    )
    adjoint = (live_mask[:, :, None] * pulled.reshape(cell_count, atom_rows, channels)).astype(
        jnp.bfloat16
    )
    row_count = M // devices
    wave_square = squared_waves(lax.axis_index("seq") * row_count, row_count)
    spectral_filter = scaled_filter(amplitude, smoothing, screening, wave_square)
    potential, source_spectra = long_range(
        charges, base_cells, cell_offsets, row_starts, spectral_filter
    )
    response, adjoint_spectra = long_range(
        adjoint, base_cells, cell_offsets, row_starts, spectral_filter
    )
    potential_rounded = potential.astype(jnp.bfloat16)
    outgoing = jnp.dot(
        potential_rounded.reshape(-1, channels), message_weight, preferred_element_type=jnp.float32
    )
    message = (live_mask[:, :, None] * outgoing.reshape(cell_count, atom_rows, features)).astype(
        jnp.bfloat16
    )
    response_rounded = (live_mask[:, :, None] * response).astype(jnp.bfloat16)
    backward = lax.dot_general(
        response_rounded.reshape(-1, channels),
        charge_weight,
        (((1,), (1,)), ((), ())),
        preferred_element_type=jnp.float32,
    )
    atom_gradient = backward.reshape(cell_count, atom_rows, features).astype(jnp.bfloat16)
    gradient_scale = 1.0 / math.sqrt(cell_count * atom_rows * devices)
    masked_cotangent = jnp.where(live_mask[:, :, None] > 0, cotangent, jnp.zeros((), jnp.bfloat16))
    gradient_in = (
        lax.dot_general(
            atom_features.reshape(-1, features),
            response_rounded.reshape(-1, channels),
            (((0,), (0,)), ((), ())),
            preferred_element_type=jnp.float32,
        )
        * gradient_scale
    )
    gradient_out = (
        lax.dot_general(
            potential_rounded.reshape(-1, channels),
            masked_cotangent.reshape(-1, features),
            (((0,), (0,)), ((), ())),
            preferred_element_type=jnp.float32,
        )
        * gradient_scale
    )
    intersection = jnp.sum(source_spectra * adjoint_spectra, axis=0) * spectral_filter
    widths = (smoothing * smoothing)[None, None, :, None]
    screens = (screening * screening)[None, None, :, None]
    smooth_factor = -widths * wave_square
    screen_factor = -2.0 * screens / (wave_square + screens)
    filter_terms = (
        jnp.stack(
            [
                jnp.sum(intersection, axis=(0, 1, 3)),
                jnp.sum(intersection * smooth_factor, axis=(0, 1, 3)),
                jnp.sum(intersection * screen_factor, axis=(0, 1, 3)),
            ]
        )
        * gradient_scale
    )
    gradient_in, gradient_out, filter_terms = lax.psum(
        (gradient_in, gradient_out, filter_terms), "seq"
    )
    return (message, atom_gradient, gradient_in, gradient_out, filter_terms)


def stacked_tables(planes):
    indices = np.arange(M)
    angles = (indices[:, None] * indices[None, :] % M) * (2.0 * np.pi / M)
    hartley = (np.cos(angles) + np.sin(angles)).astype(np.float32)
    window = (np.arange(M // planes)[:, None] * planes + np.arange(8)[None, :]) % M
    depth = hartley[:, window.reshape(-1)]

    def parts(table):
        high = table.astype(ml_dtypes.bfloat16)
        low = (table - high.astype(np.float32)).astype(ml_dtypes.bfloat16)
        return jnp.asarray(np.concatenate([high, high, low], axis=1))

    return (parts(hartley), parts(depth), parts(depth.T))


def stacked_parts(value):
    high = value.astype(jnp.bfloat16)
    low = (value - high.astype(jnp.float32)).astype(jnp.bfloat16)
    return jnp.concatenate([high, low, high], axis=0)


def wave_squares(indices):
    waves = jnp.where(indices < M // 2, indices, indices - M).astype(jnp.float32)
    return waves * waves * ((2.0 * math.pi / M) ** 2)


def mesh_kernel(
    planes,
    params_ref,
    given_ref,
    hartley_ref,
    depth_ref,
    back_ref,
    returned_ref,
    terms_ref,
    atoms_ref,
    values_ref,
    atom_planes,
    atom_columns,
    mesh,
    plane_gains,
    send_sems,
    receive_sems,
    back_sems,
    return_sems,
):
    groups, cells, unused, atoms = given_ref.shape
    lanes = 2 * M
    own = lax.axis_index("seq")
    greet_peers(groups, own)

    def send_atoms(step, carry):
        peer = lax.rem(own + step, groups)
        to_peer(
            given_ref.at[peer], atoms_ref.at[own], send_sems, receive_sems, peer, own
        ).start()
        return carry

    lax.fori_loop(1, groups, send_atoms, 0)
    atoms_ref[own] = given_ref[own]

    def spread_group(step, carry):
        group = lax.rem(own + groups - step, groups)

        @pl.when(step > 0)
        def arrive():
            to_peer(
                given_ref.at[group], atoms_ref.at[group], send_sems, receive_sems, group, group
            ).wait_recv()

        for cell in range(cells):
            places = atoms_ref[group, cell]
            fractions = spline_weights(places[3:6])
            bases = places[0:3].astype(jnp.int32)
            window = lax.broadcasted_iota(jnp.int32, (8, atoms), 0)
            along_depth = pick_weight(
                window - (bases[0:1] - group * planes), [w[0:1] for w in fractions]
            )
            index = lax.broadcasted_iota(jnp.int32, (M, atoms), 0)
            along_rows = pick_weight((index - bases[1:2]) & (M - 1), [w[1:2] for w in fractions])
            along_columns = pick_weight(
                (index - bases[2:3]) & (M - 1), [w[2:3] for w in fractions]
            )
            both = jnp.concatenate(
                [stacked_parts(along_rows), stacked_parts(along_columns)], axis=1
            )
            waves = jnp.dot(hartley_ref[...], both, preferred_element_type=jnp.float32)
            row_waves = waves[:, :atoms]
            column_waves = waves[:, atoms:]
            plane_waves = (
                (row_waves[:, None, :] * along_depth[None, :, :])
                .reshape(M * 8, atoms)
                .astype(jnp.bfloat16)
            )
            terms = jnp.concatenate(
                [column_waves * places[6:7], column_waves * places[7:8]], axis=0
            ).astype(jnp.bfloat16)
            atom_planes[group, cell] = plane_waves
            atom_columns[group, cell] = column_waves
            added = lax.dot_general(
                plane_waves, terms, (((1,), (1,)), ((), ())), preferred_element_type=jnp.float32
            )
            mesh[:, pl.ds(pl.multiple_of(group * 8, 8), 8), cell * lanes : (cell + 1) * lanes] = (
                added.reshape(M, 8, lanes)
            )
        return carry

    lax.fori_loop(0, groups, spread_group, 0)

    amplitude = params_ref[0]
    widths = params_ref[1]
    screens = params_ref[2]
    plane_squares = wave_squares(
        lax.broadcasted_iota(jnp.int32, (M, lanes), 0)
    ) + wave_squares(lax.broadcasted_iota(jnp.int32, (M, lanes), 1) & (M - 1))
    plane_gains[...] = (amplitude * (1.0 / M**3)) * jnp.exp((-0.5 * widths) * plane_squares)

    def filter_row(row, sums):
        spectrum = jnp.dot(
            depth_ref[...], stacked_parts(mesh[row]), preferred_element_type=jnp.float32
        )
        signed = jnp.where(row < M // 2, row, row - M).astype(jnp.float32)
        row_square = signed * signed * ((2.0 * math.pi / M) ** 2)
        squares = plane_squares + row_square
        screened = 1.0 / (squares + screens)
        row_gain = jnp.exp(jnp.full((1, lanes), (-0.5 * widths) * row_square, jnp.float32))
        gains = plane_gains[...] * row_gain * screened
        crossed = jnp.zeros((M, lanes), jnp.float32)
        filtered = []
        for cell in range(cells):
            part = spectrum[:, cell * lanes : (cell + 1) * lanes]
            crossed = crossed + part * pltpu.roll(part, M, 1)
            filtered.append(part * gains)
        crossed = crossed * gains
        mesh[row] = jnp.dot(
            back_ref[...],
            stacked_parts(jnp.concatenate(filtered, axis=1)),
            preferred_element_type=jnp.float32,
        )
        pieces = (crossed, crossed * squares, crossed * screened)
        return tuple(
            total + jnp.sum(piece.reshape(M // 8, 8, lanes), axis=0)
            for total, piece in zip(sums, pieces)
        )

    zero = jnp.zeros((8, lanes), jnp.float32)
    sums = lax.fori_loop(0, M, filter_row, (zero, zero, zero), unroll=4)
    for order_index in range(3):
        terms_ref[order_index] = sums[order_index]

    def read_group(step, carry):
        group = lax.rem(own + step, groups)
        for cell in range(cells):
            window = (
                mesh[
                    :, pl.ds(pl.multiple_of(group * 8, 8), 8), cell * lanes : (cell + 1) * lanes
                ]
                .reshape(M * 8, lanes)
                .astype(jnp.bfloat16)
            )
            inner = lax.dot_general(
                window,
                atom_planes[group, cell],
                (((0,), (0,)), ((), ())),
                preferred_element_type=jnp.float32,
            )
            weighted = inner.reshape(2, M, atoms) * atom_columns[group, cell][None]
            values_ref[group, cell] = jnp.sum(weighted, axis=1)

        @pl.when(step < groups)
        def give_back():
            to_peer(
                values_ref.at[group], returned_ref.at[own], back_sems, return_sems, group, own
            ).start()

        return carry

    lax.fori_loop(1, groups + 1, read_group, 0)
    returned_ref[own] = values_ref[own]

    def finish(step, carry):
        peer = lax.rem(own + groups - step, groups)
        to_peer(
            given_ref.at[peer], atoms_ref.at[peer], send_sems, receive_sems, peer, peer
        ).wait_send()
        copy = to_peer(
            values_ref.at[peer], returned_ref.at[peer], back_sems, return_sems, peer, peer
        )
        copy.wait_send()
        copy.wait_recv()
        return carry

    lax.fori_loop(1, groups, finish, 0)


def mesh_of_channel(params, atom_blocks):
    groups, cells, unused, atoms = atom_blocks.shape
    planes = M // groups
    tables = stacked_tables(planes)
    sems = pltpu.SemaphoreType.DMA((groups,))
    whole = pl.BlockSpec(memory_space=pltpu.VMEM)
    return pl.pallas_call(
        functools.partial(mesh_kernel, planes),
        out_shape=(
            jax.ShapeDtypeStruct((groups, cells, 2, atoms), jnp.float32),
            jax.ShapeDtypeStruct((3, 8, 2 * M), jnp.float32),
        ),
        in_specs=[pl.BlockSpec(memory_space=pltpu.SMEM)] + [whole] * 4,
        out_specs=(whole, whole),
        scratch_shapes=[
            pltpu.VMEM(atom_blocks.shape, jnp.float32),
            pltpu.VMEM((groups, cells, 2, atoms), jnp.float32),
            pltpu.VMEM((groups, cells, M * 8, atoms), jnp.bfloat16),
            pltpu.VMEM((groups, cells, M, atoms), jnp.float32),
            pltpu.VMEM((M, groups * 8, cells * 2 * M), jnp.float32),
            pltpu.VMEM((M, 2 * M), jnp.float32),
            sems,
            sems,
            sems,
            sems,
        ],
        compiler_params=pltpu.CompilerParams(
            collective_id=0, has_side_effects=True, vmem_limit_bytes=56 * 1024 * 1024
        ),
    )(params, atom_blocks, *tables)


def to_peer(source, target, send_sems, receive_sems, peer, sender):
    return pltpu.make_async_remote_copy(
        src_ref=source,
        dst_ref=target,
        send_sem=send_sems.at[peer],
        recv_sem=receive_sems.at[sender],
        device_id={"seq": peer},
        device_id_type=pl.DeviceIdType.MESH,
    )


def greet_peers(count, own):
    barrier = pltpu.get_barrier_semaphore()

    def greet(step, carry):
        pl.semaphore_signal(
            barrier,
            inc=1,
            device_id={"seq": lax.rem(own + step, count)},
            device_id_type=pl.DeviceIdType.MESH,
        )
        return carry

    lax.fori_loop(1, count, greet, 0)
    pl.semaphore_wait(barrier, count - 1)


def total_kernel(
    count, given_ref, fixed_ref, totals_ref, landed, send_sems, receive_sems, spread_sems, total_sems
):
    own = lax.axis_index("seq")
    greet_peers(count, own)

    def send(step, carry):
        peer = lax.rem(own + step, count)
        to_peer(given_ref.at[peer], landed.at[own], send_sems, receive_sems, peer, own).start()
        return carry

    lax.fori_loop(1, count, send, 0)

    def gather(step, total):
        peer = lax.rem(own + step, count)
        copy = to_peer(given_ref.at[peer], landed.at[peer], send_sems, receive_sems, peer, peer)
        copy.wait_send()
        copy.wait_recv()
        return total + landed[peer]

    totals_ref[own] = lax.fori_loop(1, count, gather, given_ref[own] + fixed_ref[...])

    def spread(step, carry):
        peer = lax.rem(own + step, count)
        to_peer(totals_ref.at[own], totals_ref.at[own], spread_sems, total_sems, peer, own).start()
        return carry

    lax.fori_loop(1, count, spread, 0)

    def finish(step, carry):
        peer = lax.rem(own + step, count)
        copy = to_peer(
            totals_ref.at[own], totals_ref.at[peer], spread_sems, total_sems, peer, peer
        )
        copy.wait_send()
        copy.wait_recv()
        return carry

    lax.fori_loop(1, count, finish, 0)


def totals_of_channels(blocks, fixed, collective_id):
    count = blocks.shape[0]
    whole = pl.BlockSpec(memory_space=pltpu.VMEM)
    sems = pltpu.SemaphoreType.DMA((count,))
    return pl.pallas_call(
        functools.partial(total_kernel, count),
        out_shape=jax.ShapeDtypeStruct(blocks.shape, blocks.dtype),
        in_specs=[whole, whole],
        out_specs=whole,
        scratch_shapes=[pltpu.VMEM(blocks.shape, blocks.dtype), sems, sems, sems, sems],
        compiler_params=pltpu.CompilerParams(collective_id=collective_id, has_side_effects=True),
    )(blocks, fixed)


def by_channel(
    atom_features,
    cotangent,
    charge_weight,
    message_weight,
    amplitude,
    smoothing,
    screening,
    base_cells,
    cell_offsets,
    row_starts,
    block_counts,
):
    cell_count, atom_rows, features = atom_features.shape
    channels = charge_weight.shape[1]
    devices = lax.axis_size("seq")
    blocks = block_counts.shape[1]
    channel = lax.axis_index("seq")
    slot_index = jnp.arange(atom_rows // blocks, dtype=jnp.int32)
    live = (slot_index[None, None, :] < block_counts[:, :, None]).reshape(cell_count, atom_rows)
    live_mask = live.astype(jnp.float32)
    projected = lax.dot_general(
        charge_weight,
        atom_features,
        (((0,), (2,)), ((), ())),
        preferred_element_type=jnp.float32,
    )
    pulled = lax.dot_general(
        message_weight, cotangent, (((1,), (2,)), ((), ())), preferred_element_type=jnp.float32
    )
    charges = (jnp.stack([projected, pulled], axis=2) * live_mask[None, :, None, :]).astype(
        jnp.bfloat16
    )
    places = jnp.concatenate([base_cells.astype(jnp.float32), cell_offsets], axis=1)
    blocks_out = jnp.concatenate(
        [
            jnp.broadcast_to(places[None], (devices,) + places.shape),
            charges.astype(jnp.float32),
        ],
        axis=2,
    )
    params = lax.dynamic_slice_in_dim(
        jnp.stack([amplitude, smoothing * smoothing, screening * screening]), channel, 1, 1
    ).reshape(3)
    returned, sums = mesh_of_channel(params, blocks_out)
    returned = returned.astype(jnp.bfloat16)
    potential = returned[:, :, 0]
    response = jnp.where(live[None], returned[:, :, 1], jnp.zeros((), jnp.bfloat16))
    outgoing = lax.dot_general(
        potential, message_weight, (((0,), (0,)), ((), ())), preferred_element_type=jnp.float32
    )
    message = (live_mask[:, :, None] * outgoing).astype(jnp.bfloat16)
    atom_gradient = lax.dot_general(
        response, charge_weight, (((0,), (1,)), ((), ())), preferred_element_type=jnp.float32
    ).astype(jnp.bfloat16)
    gradient_scale = 1.0 / math.sqrt(cell_count * atom_rows * devices)
    live_potential = jnp.where(live[None], potential, jnp.zeros((), jnp.bfloat16))
    gradient_in = lax.dot_general(
        response,
        atom_features,
        (((1, 2), (0, 1)), ((), ())),
        preferred_element_type=jnp.float32,
    )
    gradient_out = lax.dot_general(
        live_potential,
        cotangent,
        (((1, 2), (0, 1)), ((), ())),
        preferred_element_type=jnp.float32,
    )
    factors = jnp.stack([jnp.ones((), jnp.float32), -params[1], -2.0 * params[2]])
    own_terms = jnp.sum(sums, axis=(1, 2)) * factors * 0.5
    width = 128
    rows = features // width
    padding = 8 - 2 * rows
    blocks_out = jnp.concatenate(
        [
            gradient_in.reshape(channels, rows, width),
            gradient_out.reshape(channels, rows, width),
            jnp.zeros((channels, padding, width), jnp.float32),
        ],
        axis=1,
    )
    fixed = jnp.pad(own_terms[None, :], ((2 * rows, padding - 1), (0, width - 3)))
    totals = totals_of_channels(blocks_out, fixed, 1) * gradient_scale
    gradient_in = totals[:, :rows].reshape(channels, features).T
    gradient_out = totals[:, rows : 2 * rows].reshape(channels, features)
    filter_terms = totals[:, 2 * rows, :3].T
    return (message, atom_gradient, gradient_in, gradient_out, filter_terms)


def solution(mesh):

    def per_device(*arguments):
        by_channels = arguments[2].shape[1] == mesh.shape["seq"]
        return (by_channel if by_channels else on_device)(*arguments)

    in_specs = (
        P("groups", "seq", None),
        P("groups", "seq", None),
        P(),
        P(),
        P(),
        P(),
        P(),
        P("groups", None, "seq"),
        P("groups", None, "seq"),
        P("groups", "seq"),
        P("groups", "seq"),
    )
    out_specs = (
        P("groups", "seq", None),
        P("groups", "seq", None),
        P("groups", None),
        P("groups", None),
        P("groups", None),
    )
    return jax.shard_map(
        per_device, mesh=mesh, in_specs=in_specs, out_specs=out_specs, check_vma=False
    )
```

```python
import functools
import math

import jax
import jax.numpy as jnp
import ml_dtypes
import numpy as np
from jax import lax
from jax.experimental import pallas as pl
from jax.experimental.pallas import tpu as pltpu
from jax.sharding import PartitionSpec as P

M = 64
BAND = 32


def passed_along(value, axis, by):
    count = lax.axis_size(axis)
    return lax.ppermute(value, axis, [(i, (i + by) % count) for i in range(count)])


def spline_weights(fraction):
    remain = 1.0 - fraction
    square = fraction * fraction
    cubed = square * fraction
    return (
        remain * remain * remain / 6.0,
        (3.0 * cubed - 6.0 * square + 4.0) / 6.0,
        (-3.0 * cubed + 3.0 * square + 3.0 * fraction + 1.0) / 6.0,
        cubed / 6.0,
    )


def pick_weight(lattice_gap, weights):
    picked = jnp.where(lattice_gap == 0, weights[0], 0.0)
    for order_index in range(1, 4):
        picked = picked + jnp.where(lattice_gap == order_index, weights[order_index], 0.0)
    return picked


def atom_weights(base_cells, cell_offsets, row_start, plane_start, plane_count):
    atom_count = base_cells.shape[1]
    depth_index = plane_start + jnp.arange(plane_count, dtype=jnp.int32)
    row_index = row_start + jnp.arange(BAND, dtype=jnp.int32)
    column_index = jnp.arange(M, dtype=jnp.int32)
    along_depth = pick_weight(
        (depth_index[None, :] - base_cells[0][:, None]) % M,
        spline_weights(cell_offsets[0][:, None]),
    )
    along_rows = pick_weight(
        (row_index[None, :] - base_cells[1][:, None]) % M, spline_weights(cell_offsets[1][:, None])
    )
    along_columns = pick_weight(
        (column_index[None, :] - base_cells[2][:, None]) % M,
        spline_weights(cell_offsets[2][:, None]),
    )
    plane_rows = (
        (along_depth[:, :, None] * along_rows[:, None, :])
        .reshape(atom_count, plane_count * BAND)
        .astype(jnp.bfloat16)
    )
    return (plane_rows, along_columns)


def hartley_table():
    indices = jnp.arange(M, dtype=jnp.int32)
    product = indices[:, None] * indices[None, :] % M
    angles = product.astype(jnp.float32) * (2.0 * math.pi / M)
    return jnp.cos(angles) + jnp.sin(angles)


def wave_numbers(indices):
    return jnp.where(indices < M // 2, indices, indices - M).astype(jnp.float32) * (
        2.0 * math.pi / M
    )


def squared_waves(row_first, row_count):
    depth_waves = wave_numbers(jnp.arange(M, dtype=jnp.int32))
    row_waves = wave_numbers(row_first + jnp.arange(row_count, dtype=jnp.int32))
    summed = (
        depth_waves[:, None, None] ** 2
        + row_waves[None, :, None] ** 2
        + depth_waves[None, None, :] ** 2
    )
    return summed[:, :, None, :]


def scaled_filter(amplitude, smoothing, screening, wave_square):
    gains = amplitude[None, None, :, None]
    widths = (smoothing * smoothing)[None, None, :, None]
    screens = (screening * screening)[None, None, :, None]
    return gains * jnp.exp(-0.5 * widths * wave_square) / (wave_square + screens) * (1.0 / M**3)


def spread_cell(charges, base_cells, cell_offsets, row_starts, plane_start, plane_count):
    blocks = row_starts.shape[0]
    atom_count = charges.shape[0] // blocks
    columns = charges.shape[1] * M

    def add_block(padded, block_index):
        first_row = block_index * atom_count
        block_charges = lax.dynamic_slice_in_dim(charges, first_row, atom_count, 0)
        block_cells = lax.dynamic_slice_in_dim(base_cells, first_row, atom_count, 1)
        block_offsets = lax.dynamic_slice_in_dim(cell_offsets, first_row, atom_count, 1)
        row_start = row_starts[block_index]
        plane_rows, along_columns = atom_weights(
            block_cells, block_offsets, row_start, plane_start, plane_count
        )
        spread_rows = (
            (block_charges.astype(jnp.float32)[:, :, None] * along_columns[:, None, :])
            .reshape(atom_count, columns)
            .astype(jnp.bfloat16)
        )
        addition = lax.dot_general(
            plane_rows, spread_rows, (((0,), (0,)), ((), ())), preferred_element_type=jnp.float32
        )
        addition = addition.reshape(plane_count, BAND, columns)
        current = lax.dynamic_slice_in_dim(padded, row_start, BAND, 1)
        return (lax.dynamic_update_slice_in_dim(padded, current + addition, row_start, 1), None)

    padded = jnp.zeros((plane_count, M + BAND, columns), jnp.float32)
    padded, unused = lax.scan(add_block, padded, jnp.arange(blocks, dtype=jnp.int32))
    return padded[:, :M].at[:, :BAND].add(padded[:, M:])


def interpolate_cell(mesh, base_cells, cell_offsets, row_starts, plane_start):
    plane_count = mesh.shape[0]
    blocks = row_starts.shape[0]
    atom_count = base_cells.shape[1] // blocks
    padded = jnp.concatenate([mesh, mesh[:, :BAND]], axis=1)

    def one_block(block_index):
        first_row = block_index * atom_count
        block_cells = lax.dynamic_slice_in_dim(base_cells, first_row, atom_count, 1)
        block_offsets = lax.dynamic_slice_in_dim(cell_offsets, first_row, atom_count, 1)
        row_start = row_starts[block_index]
        plane_rows, along_columns = atom_weights(
            block_cells, block_offsets, row_start, plane_start, plane_count
        )
        window = lax.dynamic_slice_in_dim(padded, row_start, BAND, 1).reshape(
            plane_count * BAND, -1
        )
        values = jnp.dot(plane_rows, window, preferred_element_type=jnp.float32)
        return jnp.sum(values.reshape(atom_count, -1, M) * along_columns[:, None, :], axis=2)

    return lax.map(one_block, jnp.arange(blocks, dtype=jnp.int32)).reshape(blocks * atom_count, -1)


def spread_cells(charges, base_cells, cell_offsets, row_starts, plane_start, plane_count):

    def spread_one_cell(cell_data):
        return spread_cell(
            cell_data[0], cell_data[1], cell_data[2], cell_data[3], plane_start, plane_count
        )

    return lax.map(spread_one_cell, (charges, base_cells, cell_offsets, row_starts))


def interpolate_cells(mesh, base_cells, cell_offsets, row_starts, plane_start):

    def interpolate_one_cell(cell_data):
        return interpolate_cell(cell_data[0], cell_data[1], cell_data[2], cell_data[3], plane_start)

    return lax.map(interpolate_one_cell, (mesh, base_cells, cell_offsets, row_starts))


def long_range(charges, base_cells, cell_offsets, row_starts, spectral_filter):
    devices = lax.axis_size("seq")
    planes = M // devices
    spill_reach = (planes + 2) // planes
    plane_start = lax.axis_index("seq") * planes
    cell_count = charges.shape[0]
    channels = charges.shape[2]
    hartley = hartley_table()
    highest = lax.Precision.HIGHEST
    extended = spread_cells(charges, base_cells, cell_offsets, row_starts, plane_start, planes + 3)
    mesh_field = extended[:, :planes]
    for distance in range(1, spill_reach + 1):
        lower_plane = (distance - 1) * planes
        upper_plane = min(distance * planes, 3)
        arrived = passed_along(
            extended[:, planes + lower_plane : planes + upper_plane], "seq", distance
        )
        mesh_field = mesh_field.at[:, : upper_plane - lower_plane].add(arrived)
    slab_data = mesh_field.reshape(cell_count, planes, M, channels, M)
    spectrum = jnp.einsum("kpycx,xf->kpycf", slab_data, hartley, precision=highest)
    spectrum = jnp.einsum("kpycx,yf->kpfcx", spectrum, hartley, precision=highest)
    forward = jnp.einsum(
        "kzycx,zf->kfycx",
        lax.all_to_all(spectrum, "seq", split_axis=2, concat_axis=1, tiled=True),
        hartley,
        precision=highest,
    )
    weighted = spectral_filter[None] * forward
    returned = jnp.einsum("kzycx,zf->kfycx", weighted, hartley, precision=highest)
    slab_back = lax.all_to_all(returned, "seq", split_axis=1, concat_axis=2, tiled=True)
    slab_back = jnp.einsum("kpycx,yf->kpfcx", slab_back, hartley, precision=highest)
    slab_back = jnp.einsum("kpycx,xf->kpycf", slab_back, hartley, precision=highest)
    rounded = slab_back.reshape(cell_count, planes, M, channels * M).astype(jnp.bfloat16)
    pieces = [rounded]
    for distance in range(1, spill_reach + 1):
        lower_plane = (distance - 1) * planes
        upper_plane = min(distance * planes, 3)
        pieces.append(passed_along(rounded[:, : upper_plane - lower_plane], "seq", -distance))
    values = interpolate_cells(
        jnp.concatenate(pieces, axis=1), base_cells, cell_offsets, row_starts, plane_start
    )
    return (values, forward)


def on_device(
    atom_features,
    cotangent,
    charge_weight,
    message_weight,
    amplitude,
    smoothing,
    screening,
    base_cells,
    cell_offsets,
    row_starts,
    block_counts,
):
    cell_count, atom_rows, features = atom_features.shape
    channels = charge_weight.shape[1]
    devices = lax.axis_size("seq")
    blocks = block_counts.shape[1]
    slot_index = jnp.arange(atom_rows // blocks, dtype=jnp.int32)
    live_mask = (
        (slot_index[None, None, :] < block_counts[:, :, None])
        .reshape(cell_count, atom_rows)
        .astype(jnp.float32)
    )
    projected = jnp.dot(
        atom_features.reshape(-1, features), charge_weight, preferred_element_type=jnp.float32
    )
    charges = (live_mask[:, :, None] * projected.reshape(cell_count, atom_rows, channels)).astype(
        jnp.bfloat16
    )
    pulled = lax.dot_general(
        cotangent.reshape(-1, features),
        message_weight,
        (((1,), (1,)), ((), ())),
        preferred_element_type=jnp.float32,
    )
    adjoint = (live_mask[:, :, None] * pulled.reshape(cell_count, atom_rows, channels)).astype(
        jnp.bfloat16
    )
    row_count = M // devices
    wave_square = squared_waves(lax.axis_index("seq") * row_count, row_count)
    spectral_filter = scaled_filter(amplitude, smoothing, screening, wave_square)
    potential, source_spectra = long_range(
        charges, base_cells, cell_offsets, row_starts, spectral_filter
    )
    response, adjoint_spectra = long_range(
        adjoint, base_cells, cell_offsets, row_starts, spectral_filter
    )
    potential_rounded = potential.astype(jnp.bfloat16)
    outgoing = jnp.dot(
        potential_rounded.reshape(-1, channels), message_weight, preferred_element_type=jnp.float32
    )
    message = (live_mask[:, :, None] * outgoing.reshape(cell_count, atom_rows, features)).astype(
        jnp.bfloat16
    )
    response_rounded = (live_mask[:, :, None] * response).astype(jnp.bfloat16)
    backward = lax.dot_general(
        response_rounded.reshape(-1, channels),
        charge_weight,
        (((1,), (1,)), ((), ())),
        preferred_element_type=jnp.float32,
    )
    atom_gradient = backward.reshape(cell_count, atom_rows, features).astype(jnp.bfloat16)
    gradient_scale = 1.0 / math.sqrt(cell_count * atom_rows * devices)
    masked_cotangent = jnp.where(live_mask[:, :, None] > 0, cotangent, jnp.zeros((), jnp.bfloat16))
    gradient_in = (
        lax.dot_general(
            atom_features.reshape(-1, features),
            response_rounded.reshape(-1, channels),
            (((0,), (0,)), ((), ())),
            preferred_element_type=jnp.float32,
        )
        * gradient_scale
    )
    gradient_out = (
        lax.dot_general(
            potential_rounded.reshape(-1, channels),
            masked_cotangent.reshape(-1, features),
            (((0,), (0,)), ((), ())),
            preferred_element_type=jnp.float32,
        )
        * gradient_scale
    )
    intersection = jnp.sum(source_spectra * adjoint_spectra, axis=0) * spectral_filter
    widths = (smoothing * smoothing)[None, None, :, None]
    screens = (screening * screening)[None, None, :, None]
    smooth_factor = -widths * wave_square
    screen_factor = -2.0 * screens / (wave_square + screens)
    filter_terms = (
        jnp.stack(
            [
                jnp.sum(intersection, axis=(0, 1, 3)),
                jnp.sum(intersection * smooth_factor, axis=(0, 1, 3)),
                jnp.sum(intersection * screen_factor, axis=(0, 1, 3)),
            ]
        )
        * gradient_scale
    )
    gradient_in, gradient_out, filter_terms = lax.psum(
        (gradient_in, gradient_out, filter_terms), "seq"
    )
    return (message, atom_gradient, gradient_in, gradient_out, filter_terms)


def stacked_tables(planes):
    indices = np.arange(M)
    angles = (indices[:, None] * indices[None, :] % M) * (2.0 * np.pi / M)
    hartley = (np.cos(angles) + np.sin(angles)).astype(np.float32)
    window = (np.arange(M // planes)[:, None] * planes + np.arange(8)[None, :]) % M
    depth = hartley[:, window.reshape(-1)]

    def parts(table):
        high = table.astype(ml_dtypes.bfloat16)
        low = (table - high.astype(np.float32)).astype(ml_dtypes.bfloat16)
        return jnp.asarray(np.concatenate([high, high, low], axis=1))

    return (parts(hartley), parts(depth), parts(depth.T))


def stacked_parts(value):
    high = value.astype(jnp.bfloat16)
    low = (value - high.astype(jnp.float32)).astype(jnp.bfloat16)
    return jnp.concatenate([high, low, high], axis=0)


def wave_squares(indices):
    waves = jnp.where(indices < M // 2, indices, indices - M).astype(jnp.float32)
    return waves * waves * ((2.0 * math.pi / M) ** 2)


def mesh_kernel(
    planes,
    gradient_scale,
    amplitude_ref,
    smoothing_ref,
    screening_ref,
    counts_ref,
    features_ref,
    cotangent_ref,
    charge_ref,
    message_weight_ref,
    bases_ref,
    offsets_ref,
    hartley_ref,
    depth_ref,
    back_ref,
    message_ref,
    gradient_ref,
    totals_ref,
    given_ref,
    atoms_ref,
    values_ref,
    returned_ref,
    parts_ref,
    landed_ref,
    atom_planes,
    atom_columns,
    mesh,
    plane_gains,
    send_sems,
    receive_sems,
    back_sems,
    return_sems,
    part_sems,
    land_sems,
    spread_sems,
    total_sems,
):
    groups, cells, unused, atoms = given_ref.shape
    blocks = counts_ref.shape[1]
    block_atoms = atoms // blocks
    width = 128
    lanes = 2 * M
    own = lax.axis_index("seq")
    barrier = greet_peers(groups, own)
    slot = lax.broadcasted_iota(jnp.int32, (1, atoms), 1)
    live = []
    for cell in range(cells):
        mask = jnp.zeros((1, atoms), jnp.float32)
        for block in range(blocks):
            first = block * block_atoms
            held = (slot >= first) & (slot < first + counts_ref[cell, block])
            mask = jnp.where(held, 1.0, mask)
        live.append(mask)
        projected = lax.dot_general(
            charge_ref[...],
            features_ref[cell],
            (((0,), (1,)), ((), ())),
            preferred_element_type=jnp.float32,
        )
        pulled = lax.dot_general(
            message_weight_ref[...],
            cotangent_ref[cell],
            (((1,), (1,)), ((), ())),
            preferred_element_type=jnp.float32,
        )
        places = jnp.concatenate(
            [
                bases_ref[cell].astype(jnp.float32),
                offsets_ref[cell],
                jnp.zeros((2, atoms), jnp.float32),
            ],
            axis=0,
        )
        given_ref[:, cell] = placed_rows(
            [
                (6, (projected * mask).astype(jnp.bfloat16).astype(jnp.float32)),
                (7, (pulled * mask).astype(jnp.bfloat16).astype(jnp.float32)),
            ],
            jnp.broadcast_to(places[None], (groups, 8, atoms)),
        )
    pl.semaphore_wait(barrier, groups - 1)

    def send_atoms(step, carry):
        peer = lax.rem(own + step, groups)
        to_peer(
            given_ref.at[peer], atoms_ref.at[own], send_sems, receive_sems, peer, own
        ).start()
        return carry

    lax.fori_loop(1, groups, send_atoms, 0)
    atoms_ref[own] = given_ref[own]

    def spread_group(step, carry):
        group = lax.rem(own + groups - step, groups)

        @pl.when(step > 0)
        def arrive():
            to_peer(
                given_ref.at[group], atoms_ref.at[group], send_sems, receive_sems, group, group
            ).wait_recv()

        for cell in range(cells):
            places = atoms_ref[group, cell]
            fractions = spline_weights(places[3:6])
            bases = places[0:3].astype(jnp.int32)
            window = lax.broadcasted_iota(jnp.int32, (8, atoms), 0)
            along_depth = pick_weight(
                window - (bases[0:1] - group * planes), [w[0:1] for w in fractions]
            )
            index = lax.broadcasted_iota(jnp.int32, (M, atoms), 0)
            along_rows = pick_weight((index - bases[1:2]) & (M - 1), [w[1:2] for w in fractions])
            along_columns = pick_weight(
                (index - bases[2:3]) & (M - 1), [w[2:3] for w in fractions]
            )
            both = jnp.concatenate(
                [stacked_parts(along_rows), stacked_parts(along_columns)], axis=1
            )
            waves = jnp.dot(hartley_ref[...], both, preferred_element_type=jnp.float32)
            row_waves = waves[:, :atoms]
            column_waves = waves[:, atoms:]
            plane_waves = (
                (row_waves[:, None, :] * along_depth[None, :, :])
                .reshape(M * 8, atoms)
                .astype(jnp.bfloat16)
            )
            terms = jnp.concatenate(
                [column_waves * places[6:7], column_waves * places[7:8]], axis=0
            ).astype(jnp.bfloat16)
            atom_planes[group, cell] = plane_waves
            atom_columns[group, cell] = column_waves
            added = lax.dot_general(
                plane_waves, terms, (((1,), (1,)), ((), ())), preferred_element_type=jnp.float32
            )
            mesh[:, pl.ds(pl.multiple_of(group * 8, 8), 8), cell * lanes : (cell + 1) * lanes] = (
                added.reshape(M, 8, lanes)
            )
        return carry

    lax.fori_loop(0, groups, spread_group, 0)

    amplitude = amplitude_ref[own]
    widths = smoothing_ref[own] * smoothing_ref[own]
    screens = screening_ref[own] * screening_ref[own]
    plane_squares = wave_squares(
        lax.broadcasted_iota(jnp.int32, (M, lanes), 0)
    ) + wave_squares(lax.broadcasted_iota(jnp.int32, (M, lanes), 1) & (M - 1))
    plane_gains[...] = (amplitude * (1.0 / M**3)) * jnp.exp((-0.5 * widths) * plane_squares)

    def filter_row(row, sums):
        spectrum = jnp.dot(
            depth_ref[...], stacked_parts(mesh[row]), preferred_element_type=jnp.float32
        )
        signed = jnp.where(row < M // 2, row, row - M).astype(jnp.float32)
        row_square = signed * signed * ((2.0 * math.pi / M) ** 2)
        squares = plane_squares + row_square
        screened = 1.0 / (squares + screens)
        row_gain = jnp.exp(jnp.full((1, lanes), (-0.5 * widths) * row_square, jnp.float32))
        gains = plane_gains[...] * row_gain * screened
        crossed = jnp.zeros((M, lanes), jnp.float32)
        filtered = []
        for cell in range(cells):
            part = spectrum[:, cell * lanes : (cell + 1) * lanes]
            crossed = crossed + part * pltpu.roll(part, M, 1)
            filtered.append(part * gains)
        crossed = crossed * gains
        mesh[row] = jnp.dot(
            back_ref[...],
            stacked_parts(jnp.concatenate(filtered, axis=1)),
            preferred_element_type=jnp.float32,
        )
        pieces = (crossed, crossed * squares, crossed * screened)
        return tuple(
            total + jnp.sum(piece.reshape(M // 8, 8, lanes), axis=0)
            for total, piece in zip(sums, pieces)
        )

    zero = jnp.zeros((8, lanes), jnp.float32)
    sums = lax.fori_loop(0, M, filter_row, (zero, zero, zero), unroll=4)
    own_terms = [
        jnp.sum(jnp.sum(total, axis=0, keepdims=True), axis=1, keepdims=True) * factor
        for total, factor in zip(sums, (0.5, -0.5 * widths, -screens))
    ]

    def read_group(step, carry):
        group = lax.rem(own + step, groups)
        for cell in range(cells):
            window = (
                mesh[
                    :, pl.ds(pl.multiple_of(group * 8, 8), 8), cell * lanes : (cell + 1) * lanes
                ]
                .reshape(M * 8, lanes)
                .astype(jnp.bfloat16)
            )
            inner = lax.dot_general(
                window,
                atom_planes[group, cell],
                (((0,), (0,)), ((), ())),
                preferred_element_type=jnp.float32,
            )
            weighted = inner.reshape(2, M, atoms) * atom_columns[group, cell][None]
            values_ref[group, 2 * cell : 2 * cell + 2] = jnp.sum(weighted, axis=1)

        @pl.when(step < groups)
        def give_back():
            to_peer(
                values_ref.at[group], returned_ref.at[own], back_sems, return_sems, group, own
            ).start()

        return carry

    lax.fori_loop(1, groups + 1, read_group, 0)
    returned_ref[own] = values_ref[own]

    def finish(step, carry):
        peer = lax.rem(own + groups - step, groups)
        to_peer(
            given_ref.at[peer], atoms_ref.at[peer], send_sems, receive_sems, peer, peer
        ).wait_send()
        copy = to_peer(
            values_ref.at[peer], returned_ref.at[peer], back_sems, return_sems, peer, peer
        )
        copy.wait_send()
        copy.wait_recv()
        return carry

    lax.fori_loop(1, groups, finish, 0)

    returned = jnp.concatenate([returned_ref[index] for index in range(groups)], axis=0).astype(
        jnp.bfloat16
    )
    kinds = 2 * cells
    picked_row = lax.broadcasted_iota(jnp.int32, (groups, groups * kinds), 1)
    channel_row = lax.broadcasted_iota(jnp.int32, (groups, groups * kinds), 0) * kinds

    def kind_of(cell, kind):
        picker = jnp.where(picked_row == channel_row + (2 * cell + kind), 1.0, 0.0)
        picked = jnp.dot(
            picker.astype(jnp.bfloat16), returned, preferred_element_type=jnp.float32
        )
        return (picked * live[cell]).astype(jnp.bfloat16)

    potentials = [kind_of(cell, 0) for cell in range(cells)]
    responses = [kind_of(cell, 1) for cell in range(cells)]
    gradient_in = jnp.zeros((groups, features_ref.shape[2]), jnp.float32)
    gradient_out = gradient_in
    for cell in range(cells):
        gradient_in = gradient_in + jnp.dot(
            responses[cell], features_ref[cell], preferred_element_type=jnp.float32
        )
        gradient_out = gradient_out + jnp.dot(
            potentials[cell], cotangent_ref[cell], preferred_element_type=jnp.float32
        )
    parts_ref[...] = placed_rows(
        [
            (0, gradient_in[:, :width]),
            (1, gradient_in[:, width:]),
            (2, gradient_out[:, :width]),
            (3, gradient_out[:, width:]),
        ],
        jnp.zeros(parts_ref.shape, jnp.float32),
    )

    def send_parts(step, carry):
        peer = lax.rem(own + step, groups)
        to_peer(
            parts_ref.at[peer], landed_ref.at[own], part_sems, land_sems, peer, own
        ).start()
        return carry

    lax.fori_loop(1, groups, send_parts, 0)
    for cell in range(cells):
        message_ref[cell] = lax.dot_general(
            potentials[cell],
            message_weight_ref[...],
            (((0,), (0,)), ((), ())),
            preferred_element_type=jnp.float32,
        ).astype(jnp.bfloat16)
        gradient_ref[cell] = lax.dot_general(
            responses[cell],
            charge_ref[...],
            (((0,), (1,)), ((), ())),
            preferred_element_type=jnp.float32,
        ).astype(jnp.bfloat16)
    row_index = lax.broadcasted_iota(jnp.int32, (8, width), 0)
    lane_index = lax.broadcasted_iota(jnp.int32, (8, width), 1)
    fixed = jnp.zeros((8, width), jnp.float32)
    for order_index in range(3):
        fixed = jnp.where(
            (row_index == 4) & (lane_index == order_index), own_terms[order_index], fixed
        )

    def gather_parts(step, total):
        peer = lax.rem(own + groups - step, groups)
        copy = to_peer(
            parts_ref.at[peer], landed_ref.at[peer], part_sems, land_sems, peer, peer
        )
        copy.wait_send()
        copy.wait_recv()
        return total + landed_ref[peer]

    totals_ref[own] = (
        lax.fori_loop(1, groups, gather_parts, parts_ref[own] + fixed) * gradient_scale
    )

    def spread_totals(step, carry):
        peer = lax.rem(own + step, groups)
        to_peer(
            totals_ref.at[own], totals_ref.at[own], spread_sems, total_sems, peer, own
        ).start()
        return carry

    lax.fori_loop(1, groups, spread_totals, 0)

    def finish_totals(step, carry):
        peer = lax.rem(own + groups - step, groups)
        copy = to_peer(
            totals_ref.at[own], totals_ref.at[peer], spread_sems, total_sems, peer, peer
        )
        copy.wait_send()
        copy.wait_recv()
        return carry

    lax.fori_loop(1, groups, finish_totals, 0)


def to_peer(source, target, send_sems, receive_sems, peer, sender):
    return pltpu.make_async_remote_copy(
        src_ref=source,
        dst_ref=target,
        send_sem=send_sems.at[peer],
        recv_sem=receive_sems.at[sender],
        device_id={"seq": peer},
        device_id_type=pl.DeviceIdType.MESH,
    )


def greet_peers(count, own):
    barrier = pltpu.get_barrier_semaphore()

    def greet(step, carry):
        pl.semaphore_signal(
            barrier,
            inc=1,
            device_id={"seq": lax.rem(own + step, count)},
            device_id_type=pl.DeviceIdType.MESH,
        )
        return carry

    lax.fori_loop(1, count, greet, 0)
    return barrier


def placed_rows(entries, base):
    row_index = lax.broadcasted_iota(jnp.int32, base.shape, 1)
    for row, table in entries:
        base = jnp.where(row_index == row, table[:, None, :], base)
    return base


def by_channel(
    atom_features,
    cotangent,
    charge_weight,
    message_weight,
    amplitude,
    smoothing,
    screening,
    base_cells,
    cell_offsets,
    row_starts,
    block_counts,
):
    cells, atoms, features = atom_features.shape
    groups = charge_weight.shape[1]
    planes = M // groups
    tables = stacked_tables(planes)
    sems = pltpu.SemaphoreType.DMA((groups,))
    whole = pl.BlockSpec(memory_space=pltpu.VMEM)
    scalar = pl.BlockSpec(memory_space=pltpu.SMEM)
    gradient_scale = 1.0 / math.sqrt(cells * atoms * groups)
    atom_blocks = (groups, cells, 8, atoms)
    value_blocks = (groups, 2 * cells, atoms)
    part_blocks = (groups, 8, 128)
    message, atom_gradient, totals = pl.pallas_call(
        functools.partial(mesh_kernel, planes, gradient_scale),
        out_shape=(
            jax.ShapeDtypeStruct(atom_features.shape, jnp.bfloat16),
            jax.ShapeDtypeStruct(atom_features.shape, jnp.bfloat16),
            jax.ShapeDtypeStruct(part_blocks, jnp.float32),
        ),
        in_specs=[scalar] * 4 + [whole] * 9,
        out_specs=(whole, whole, whole),
        scratch_shapes=[
            pltpu.VMEM(atom_blocks, jnp.float32),
            pltpu.VMEM(atom_blocks, jnp.float32),
            pltpu.VMEM(value_blocks, jnp.float32),
            pltpu.VMEM(value_blocks, jnp.float32),
            pltpu.VMEM(part_blocks, jnp.float32),
            pltpu.VMEM(part_blocks, jnp.float32),
            pltpu.VMEM((groups, cells, M * 8, atoms), jnp.bfloat16),
            pltpu.VMEM((groups, cells, M, atoms), jnp.float32),
            pltpu.VMEM((M, groups * 8, cells * 2 * M), jnp.float32),
            pltpu.VMEM((M, 2 * M), jnp.float32),
        ]
        + [sems] * 8,
        compiler_params=pltpu.CompilerParams(
            collective_id=0, has_side_effects=True, vmem_limit_bytes=56 * 1024 * 1024
        ),
    )(
        amplitude,
        smoothing,
        screening,
        block_counts,
        atom_features,
        cotangent,
        charge_weight,
        message_weight,
        base_cells,
        cell_offsets,
        *tables,
    )
    gradient_in = totals[:, 0:2].reshape(groups, features).T
    gradient_out = totals[:, 2:4].reshape(groups, features)
    filter_terms = totals[:, 4, :3].T
    return (message, atom_gradient, gradient_in, gradient_out, filter_terms)


def solution(mesh):

    def per_device(*arguments):
        by_channels = arguments[2].shape[1] == mesh.shape["seq"]
        return (by_channel if by_channels else on_device)(*arguments)

    in_specs = (
        P("groups", "seq", None),
        P("groups", "seq", None),
        P(),
        P(),
        P(),
        P(),
        P(),
        P("groups", None, "seq"),
        P("groups", None, "seq"),
        P("groups", "seq"),
        P("groups", "seq"),
    )
    out_specs = (
        P("groups", "seq", None),
        P("groups", "seq", None),
        P("groups", None),
        P("groups", None),
        P("groups", None),
    )
    return jax.shard_map(
        per_device, mesh=mesh, in_specs=in_specs, out_specs=out_specs, check_vma=False
    )
```

```python
import functools
import math

import jax
import jax.numpy as jnp
import ml_dtypes
import numpy as np
from jax import lax
from jax.experimental import pallas as pl
from jax.experimental.pallas import tpu as pltpu
from jax.sharding import PartitionSpec as P

M = 64
BAND = 32


def passed_along(value, axis, by):
    count = lax.axis_size(axis)
    return lax.ppermute(value, axis, [(i, (i + by) % count) for i in range(count)])


def spline_weights(fraction):
    remain = 1.0 - fraction
    square = fraction * fraction
    cubed = square * fraction
    return (
        remain * remain * remain / 6.0,
        (3.0 * cubed - 6.0 * square + 4.0) / 6.0,
        (-3.0 * cubed + 3.0 * square + 3.0 * fraction + 1.0) / 6.0,
        cubed / 6.0,
    )


def pick_weight(lattice_gap, weights):
    picked = jnp.where(lattice_gap == 0, weights[0], 0.0)
    for order_index in range(1, 4):
        picked = picked + jnp.where(lattice_gap == order_index, weights[order_index], 0.0)
    return picked


def atom_weights(base_cells, cell_offsets, row_start, plane_start, plane_count):
    atom_count = base_cells.shape[1]
    depth_index = plane_start + jnp.arange(plane_count, dtype=jnp.int32)
    row_index = row_start + jnp.arange(BAND, dtype=jnp.int32)
    column_index = jnp.arange(M, dtype=jnp.int32)
    along_depth = pick_weight(
        (depth_index[None, :] - base_cells[0][:, None]) % M,
        spline_weights(cell_offsets[0][:, None]),
    )
    along_rows = pick_weight(
        (row_index[None, :] - base_cells[1][:, None]) % M, spline_weights(cell_offsets[1][:, None])
    )
    along_columns = pick_weight(
        (column_index[None, :] - base_cells[2][:, None]) % M,
        spline_weights(cell_offsets[2][:, None]),
    )
    plane_rows = (
        (along_depth[:, :, None] * along_rows[:, None, :])
        .reshape(atom_count, plane_count * BAND)
        .astype(jnp.bfloat16)
    )
    return (plane_rows, along_columns)


def hartley_table():
    indices = jnp.arange(M, dtype=jnp.int32)
    product = indices[:, None] * indices[None, :] % M
    angles = product.astype(jnp.float32) * (2.0 * math.pi / M)
    return jnp.cos(angles) + jnp.sin(angles)


def wave_numbers(indices):
    return jnp.where(indices < M // 2, indices, indices - M).astype(jnp.float32) * (
        2.0 * math.pi / M
    )


def squared_waves(row_first, row_count):
    depth_waves = wave_numbers(jnp.arange(M, dtype=jnp.int32))
    row_waves = wave_numbers(row_first + jnp.arange(row_count, dtype=jnp.int32))
    summed = (
        depth_waves[:, None, None] ** 2
        + row_waves[None, :, None] ** 2
        + depth_waves[None, None, :] ** 2
    )
    return summed[:, :, None, :]


def scaled_filter(amplitude, smoothing, screening, wave_square):
    gains = amplitude[None, None, :, None]
    widths = (smoothing * smoothing)[None, None, :, None]
    screens = (screening * screening)[None, None, :, None]
    return gains * jnp.exp(-0.5 * widths * wave_square) / (wave_square + screens) * (1.0 / M**3)


def spread_cell(charges, base_cells, cell_offsets, row_starts, plane_start, plane_count):
    blocks = row_starts.shape[0]
    atom_count = charges.shape[0] // blocks
    columns = charges.shape[1] * M

    def add_block(padded, block_index):
        first_row = block_index * atom_count
        block_charges = lax.dynamic_slice_in_dim(charges, first_row, atom_count, 0)
        block_cells = lax.dynamic_slice_in_dim(base_cells, first_row, atom_count, 1)
        block_offsets = lax.dynamic_slice_in_dim(cell_offsets, first_row, atom_count, 1)
        row_start = row_starts[block_index]
        plane_rows, along_columns = atom_weights(
            block_cells, block_offsets, row_start, plane_start, plane_count
        )
        spread_rows = (
            (block_charges.astype(jnp.float32)[:, :, None] * along_columns[:, None, :])
            .reshape(atom_count, columns)
            .astype(jnp.bfloat16)
        )
        addition = lax.dot_general(
            plane_rows, spread_rows, (((0,), (0,)), ((), ())), preferred_element_type=jnp.float32
        )
        addition = addition.reshape(plane_count, BAND, columns)
        current = lax.dynamic_slice_in_dim(padded, row_start, BAND, 1)
        return (lax.dynamic_update_slice_in_dim(padded, current + addition, row_start, 1), None)

    padded = jnp.zeros((plane_count, M + BAND, columns), jnp.float32)
    padded, unused = lax.scan(add_block, padded, jnp.arange(blocks, dtype=jnp.int32))
    return padded[:, :M].at[:, :BAND].add(padded[:, M:])


def interpolate_cell(mesh, base_cells, cell_offsets, row_starts, plane_start):
    plane_count = mesh.shape[0]
    blocks = row_starts.shape[0]
    atom_count = base_cells.shape[1] // blocks
    padded = jnp.concatenate([mesh, mesh[:, :BAND]], axis=1)

    def one_block(block_index):
        first_row = block_index * atom_count
        block_cells = lax.dynamic_slice_in_dim(base_cells, first_row, atom_count, 1)
        block_offsets = lax.dynamic_slice_in_dim(cell_offsets, first_row, atom_count, 1)
        row_start = row_starts[block_index]
        plane_rows, along_columns = atom_weights(
            block_cells, block_offsets, row_start, plane_start, plane_count
        )
        window = lax.dynamic_slice_in_dim(padded, row_start, BAND, 1).reshape(
            plane_count * BAND, -1
        )
        values = jnp.dot(plane_rows, window, preferred_element_type=jnp.float32)
        return jnp.sum(values.reshape(atom_count, -1, M) * along_columns[:, None, :], axis=2)

    return lax.map(one_block, jnp.arange(blocks, dtype=jnp.int32)).reshape(blocks * atom_count, -1)


def spread_cells(charges, base_cells, cell_offsets, row_starts, plane_start, plane_count):

    def spread_one_cell(cell_data):
        return spread_cell(
            cell_data[0], cell_data[1], cell_data[2], cell_data[3], plane_start, plane_count
        )

    return lax.map(spread_one_cell, (charges, base_cells, cell_offsets, row_starts))


def interpolate_cells(mesh, base_cells, cell_offsets, row_starts, plane_start):

    def interpolate_one_cell(cell_data):
        return interpolate_cell(cell_data[0], cell_data[1], cell_data[2], cell_data[3], plane_start)

    return lax.map(interpolate_one_cell, (mesh, base_cells, cell_offsets, row_starts))


def long_range(charges, base_cells, cell_offsets, row_starts, spectral_filter):
    devices = lax.axis_size("seq")
    planes = M // devices
    spill_reach = (planes + 2) // planes
    plane_start = lax.axis_index("seq") * planes
    cell_count = charges.shape[0]
    channels = charges.shape[2]
    hartley = hartley_table()
    highest = lax.Precision.HIGHEST
    extended = spread_cells(charges, base_cells, cell_offsets, row_starts, plane_start, planes + 3)
    mesh_field = extended[:, :planes]
    for distance in range(1, spill_reach + 1):
        lower_plane = (distance - 1) * planes
        upper_plane = min(distance * planes, 3)
        arrived = passed_along(
            extended[:, planes + lower_plane : planes + upper_plane], "seq", distance
        )
        mesh_field = mesh_field.at[:, : upper_plane - lower_plane].add(arrived)
    slab_data = mesh_field.reshape(cell_count, planes, M, channels, M)
    spectrum = jnp.einsum("kpycx,xf->kpycf", slab_data, hartley, precision=highest)
    spectrum = jnp.einsum("kpycx,yf->kpfcx", spectrum, hartley, precision=highest)
    forward = jnp.einsum(
        "kzycx,zf->kfycx",
        lax.all_to_all(spectrum, "seq", split_axis=2, concat_axis=1, tiled=True),
        hartley,
        precision=highest,
    )
    weighted = spectral_filter[None] * forward
    returned = jnp.einsum("kzycx,zf->kfycx", weighted, hartley, precision=highest)
    slab_back = lax.all_to_all(returned, "seq", split_axis=1, concat_axis=2, tiled=True)
    slab_back = jnp.einsum("kpycx,yf->kpfcx", slab_back, hartley, precision=highest)
    slab_back = jnp.einsum("kpycx,xf->kpycf", slab_back, hartley, precision=highest)
    rounded = slab_back.reshape(cell_count, planes, M, channels * M).astype(jnp.bfloat16)
    pieces = [rounded]
    for distance in range(1, spill_reach + 1):
        lower_plane = (distance - 1) * planes
        upper_plane = min(distance * planes, 3)
        pieces.append(passed_along(rounded[:, : upper_plane - lower_plane], "seq", -distance))
    values = interpolate_cells(
        jnp.concatenate(pieces, axis=1), base_cells, cell_offsets, row_starts, plane_start
    )
    return (values, forward)


def on_device(
    atom_features,
    cotangent,
    charge_weight,
    message_weight,
    amplitude,
    smoothing,
    screening,
    base_cells,
    cell_offsets,
    row_starts,
    block_counts,
):
    cell_count, atom_rows, features = atom_features.shape
    channels = charge_weight.shape[1]
    devices = lax.axis_size("seq")
    blocks = block_counts.shape[1]
    slot_index = jnp.arange(atom_rows // blocks, dtype=jnp.int32)
    live_mask = (
        (slot_index[None, None, :] < block_counts[:, :, None])
        .reshape(cell_count, atom_rows)
        .astype(jnp.float32)
    )
    projected = jnp.dot(
        atom_features.reshape(-1, features), charge_weight, preferred_element_type=jnp.float32
    )
    charges = (live_mask[:, :, None] * projected.reshape(cell_count, atom_rows, channels)).astype(
        jnp.bfloat16
    )
    pulled = lax.dot_general(
        cotangent.reshape(-1, features),
        message_weight,
        (((1,), (1,)), ((), ())),
        preferred_element_type=jnp.float32,
    )
    adjoint = (live_mask[:, :, None] * pulled.reshape(cell_count, atom_rows, channels)).astype(
        jnp.bfloat16
    )
    row_count = M // devices
    wave_square = squared_waves(lax.axis_index("seq") * row_count, row_count)
    spectral_filter = scaled_filter(amplitude, smoothing, screening, wave_square)
    potential, source_spectra = long_range(
        charges, base_cells, cell_offsets, row_starts, spectral_filter
    )
    response, adjoint_spectra = long_range(
        adjoint, base_cells, cell_offsets, row_starts, spectral_filter
    )
    potential_rounded = potential.astype(jnp.bfloat16)
    outgoing = jnp.dot(
        potential_rounded.reshape(-1, channels), message_weight, preferred_element_type=jnp.float32
    )
    message = (live_mask[:, :, None] * outgoing.reshape(cell_count, atom_rows, features)).astype(
        jnp.bfloat16
    )
    response_rounded = (live_mask[:, :, None] * response).astype(jnp.bfloat16)
    backward = lax.dot_general(
        response_rounded.reshape(-1, channels),
        charge_weight,
        (((1,), (1,)), ((), ())),
        preferred_element_type=jnp.float32,
    )
    atom_gradient = backward.reshape(cell_count, atom_rows, features).astype(jnp.bfloat16)
    gradient_scale = 1.0 / math.sqrt(cell_count * atom_rows * devices)
    masked_cotangent = jnp.where(live_mask[:, :, None] > 0, cotangent, jnp.zeros((), jnp.bfloat16))
    gradient_in = (
        lax.dot_general(
            atom_features.reshape(-1, features),
            response_rounded.reshape(-1, channels),
            (((0,), (0,)), ((), ())),
            preferred_element_type=jnp.float32,
        )
        * gradient_scale
    )
    gradient_out = (
        lax.dot_general(
            potential_rounded.reshape(-1, channels),
            masked_cotangent.reshape(-1, features),
            (((0,), (0,)), ((), ())),
            preferred_element_type=jnp.float32,
        )
        * gradient_scale
    )
    intersection = jnp.sum(source_spectra * adjoint_spectra, axis=0) * spectral_filter
    widths = (smoothing * smoothing)[None, None, :, None]
    screens = (screening * screening)[None, None, :, None]
    smooth_factor = -widths * wave_square
    screen_factor = -2.0 * screens / (wave_square + screens)
    filter_terms = (
        jnp.stack(
            [
                jnp.sum(intersection, axis=(0, 1, 3)),
                jnp.sum(intersection * smooth_factor, axis=(0, 1, 3)),
                jnp.sum(intersection * screen_factor, axis=(0, 1, 3)),
            ]
        )
        * gradient_scale
    )
    gradient_in, gradient_out, filter_terms = lax.psum(
        (gradient_in, gradient_out, filter_terms), "seq"
    )
    return (message, atom_gradient, gradient_in, gradient_out, filter_terms)


def stacked_tables(planes):
    indices = np.arange(M)
    angles = (indices[:, None] * indices[None, :] % M) * (2.0 * np.pi / M)
    hartley = (np.cos(angles) + np.sin(angles)).astype(np.float32)
    window = (np.arange(M // planes)[:, None] * planes + np.arange(8)[None, :]) % M
    depth = hartley[:, window.reshape(-1)]

    def parts(table):
        high = table.astype(ml_dtypes.bfloat16)
        low = (table - high.astype(np.float32)).astype(ml_dtypes.bfloat16)
        return np.concatenate([high, high, low], axis=1)

    high, unused, low = np.split(parts(depth), 3, axis=1)
    stacked_depth = np.concatenate([high, low], axis=0)
    return tuple(jnp.asarray(table) for table in (parts(hartley), stacked_depth, parts(depth.T)))


def stacked_parts(value):
    high = value.astype(jnp.bfloat16)
    low = (value - high.astype(jnp.float32)).astype(jnp.bfloat16)
    return jnp.concatenate([high, low, high], axis=0)


def wave_squares(indices):
    waves = jnp.where(indices < M // 2, indices, indices - M).astype(jnp.float32)
    return waves * waves * ((2.0 * math.pi / M) ** 2)


def mesh_kernel(
    planes,
    gradient_scale,
    amplitude_ref,
    smoothing_ref,
    screening_ref,
    counts_ref,
    features_ref,
    cotangent_ref,
    charge_ref,
    message_weight_ref,
    bases_ref,
    offsets_ref,
    hartley_ref,
    depth_ref,
    back_ref,
    message_ref,
    gradient_ref,
    totals_ref,
    given_ref,
    atoms_ref,
    values_ref,
    returned_ref,
    parts_ref,
    landed_ref,
    atom_planes,
    atom_columns,
    mesh,
    plane_gains,
    send_sems,
    receive_sems,
    back_sems,
    return_sems,
    part_sems,
    land_sems,
    spread_sems,
    total_sems,
):
    groups, cells, unused, atoms = given_ref.shape
    blocks = counts_ref.shape[1]
    block_atoms = atoms // blocks
    width = 128
    lanes = 2 * M
    own = lax.axis_index("seq")
    barrier = greet_peers(groups, own)
    slot = lax.broadcasted_iota(jnp.int32, (1, atoms), 1)
    live = []
    for cell in range(cells):
        mask = jnp.zeros((1, atoms), jnp.float32)
        for block in range(blocks):
            first = block * block_atoms
            held = (slot >= first) & (slot < first + counts_ref[cell, block])
            mask = jnp.where(held, 1.0, mask)
        live.append(mask)
        projected = lax.dot_general(
            charge_ref[...],
            features_ref[cell],
            (((1,), (1,)), ((), ())),
            preferred_element_type=jnp.float32,
        )
        pulled = lax.dot_general(
            message_weight_ref[...],
            cotangent_ref[cell],
            (((1,), (1,)), ((), ())),
            preferred_element_type=jnp.float32,
        )
        places = jnp.concatenate(
            [
                *(bases_ref[way, cell : cell + 1].astype(jnp.float32) for way in range(3)),
                *(offsets_ref[way, cell : cell + 1] for way in range(3)),
                jnp.zeros((2, atoms), jnp.float32),
            ],
            axis=0,
        )
        given_ref[:, cell] = placed_rows(
            [
                (6, (projected * mask).astype(jnp.bfloat16).astype(jnp.float32)),
                (7, (pulled * mask).astype(jnp.bfloat16).astype(jnp.float32)),
            ],
            jnp.broadcast_to(places[None], (groups, 8, atoms)),
        )
    pl.semaphore_wait(barrier, groups - 1)

    def send_atoms(step, carry):
        peer = lax.rem(own + step, groups)
        to_peer(
            given_ref.at[peer], atoms_ref.at[own], send_sems, receive_sems, peer, own
        ).start()
        return carry

    lax.fori_loop(1, groups, send_atoms, 0)
    atoms_ref[own] = given_ref[own]

    def spread_group(group):
        for cell in range(cells):
            places = atoms_ref[group, cell]
            fractions = spline_weights(places[3:6])
            bases = places[0:3].astype(jnp.int32)
            window = lax.broadcasted_iota(jnp.int32, (8, atoms), 0)
            along_depth = pick_weight(
                window - (bases[0:1] - group * planes), [w[0:1] for w in fractions]
            )
            index = lax.broadcasted_iota(jnp.int32, (M, atoms), 0)
            along_rows = pick_weight((index - bases[1:2]) & (M - 1), [w[1:2] for w in fractions])
            along_columns = pick_weight(
                (index - bases[2:3]) & (M - 1), [w[2:3] for w in fractions]
            )
            both = jnp.concatenate(
                [stacked_parts(along_rows), stacked_parts(along_columns)], axis=1
            )
            waves = jnp.dot(hartley_ref[...], both, preferred_element_type=jnp.float32)
            row_waves = waves[:, :atoms]
            column_waves = waves[:, atoms:]
            plane_waves = (
                (row_waves[:, None, :] * along_depth[None, :, :])
                .reshape(M * 8, atoms)
                .astype(jnp.bfloat16)
            )
            terms = jnp.concatenate(
                [column_waves * places[6:7], column_waves * places[7:8]], axis=0
            ).astype(jnp.bfloat16)
            atom_planes[group, cell] = plane_waves
            atom_columns[group, cell] = column_waves
            added = lax.dot_general(
                plane_waves, terms, (((1,), (1,)), ((), ())), preferred_element_type=jnp.float32
            )
            mesh[:, pl.ds(pl.multiple_of(group * 8, 8), 8), cell * lanes : (cell + 1) * lanes] = (
                added.reshape(M, 8, lanes)
            )

    spread_group(own)
    together = 3 if groups % 3 == 1 else 1

    def spread_groups(step, carry):
        arrived = [
            lax.rem(own + groups - (1 + step * together + ahead), groups)
            for ahead in range(together)
        ]
        for group in arrived:
            to_peer(
                given_ref.at[group], atoms_ref.at[group], send_sems, receive_sems, group, group
            ).wait_recv()
        for group in arrived:
            spread_group(group)
        return carry

    lax.fori_loop(0, (groups - 1) // together, spread_groups, 0)

    amplitude = amplitude_ref[own]
    widths = smoothing_ref[own] * smoothing_ref[own]
    screens = screening_ref[own] * screening_ref[own]
    plane_squares = wave_squares(
        lax.broadcasted_iota(jnp.int32, (M, lanes), 0)
    ) + wave_squares(lax.broadcasted_iota(jnp.int32, (M, lanes), 1) & (M - 1))
    plane_gains[...] = (amplitude * (1.0 / M**3)) * jnp.exp((-0.5 * widths) * plane_squares)

    def filter_row(row, sums):
        both = jnp.dot(
            depth_ref[...], mesh[row].astype(jnp.bfloat16), preferred_element_type=jnp.float32
        )
        spectrum = both[:M] + both[M:]
        signed = jnp.where(row < M // 2, row, row - M).astype(jnp.float32)
        row_square = signed * signed * ((2.0 * math.pi / M) ** 2)
        squares = plane_squares + row_square
        screened = 1.0 / (squares + screens)
        row_gain = jnp.exp(jnp.full((1, lanes), (-0.5 * widths) * row_square, jnp.float32))
        gains = plane_gains[...] * row_gain * screened
        crossed = jnp.zeros((M, lanes), jnp.float32)
        filtered = []
        for cell in range(cells):
            part = spectrum[:, cell * lanes : (cell + 1) * lanes]
            crossed = crossed + part * pltpu.roll(part, M, 1)
            filtered.append(part * gains)
        crossed = crossed * gains
        mesh[row] = jnp.dot(
            back_ref[...],
            stacked_parts(jnp.concatenate(filtered, axis=1)),
            preferred_element_type=jnp.float32,
        )
        pieces = (crossed, crossed * squares, crossed * screened)
        return tuple(
            total + jnp.sum(piece.reshape(M // 8, 8, lanes), axis=0)
            for total, piece in zip(sums, pieces)
        )

    zero = jnp.zeros((8, lanes), jnp.float32)
    sums = lax.fori_loop(0, M, filter_row, (zero, zero, zero), unroll=8)
    own_terms = [
        jnp.sum(jnp.sum(total, axis=0, keepdims=True), axis=1, keepdims=True) * factor
        for total, factor in zip(sums, (0.5, -0.5 * widths, -screens))
    ]

    def read_group(group):
        for cell in range(cells):
            window = (
                mesh[
                    :, pl.ds(pl.multiple_of(group * 8, 8), 8), cell * lanes : (cell + 1) * lanes
                ]
                .reshape(M * 8, lanes)
                .astype(jnp.bfloat16)
            )
            inner = lax.dot_general(
                window,
                atom_planes[group, cell],
                (((0,), (0,)), ((), ())),
                preferred_element_type=jnp.float32,
            )
            weighted = inner.reshape(2, M, atoms) * atom_columns[group, cell][None]
            values_ref[group, 2 * cell : 2 * cell + 2] = jnp.sum(weighted, axis=1)

    def read_groups(step, carry):
        asked = [
            lax.rem(own + (1 + step * together + ahead), groups) for ahead in range(together)
        ]
        for group in asked:
            read_group(group)
        for group in asked:
            to_peer(
                values_ref.at[group], returned_ref.at[own], back_sems, return_sems, group, own
            ).start()
        return carry

    lax.fori_loop(0, (groups - 1) // together, read_groups, 0)
    read_group(own)
    returned_ref[own] = values_ref[own]

    def finish(step, carry):
        peer = lax.rem(own + groups - step, groups)
        to_peer(
            given_ref.at[peer], atoms_ref.at[peer], send_sems, receive_sems, peer, peer
        ).wait_send()
        copy = to_peer(
            values_ref.at[peer], returned_ref.at[peer], back_sems, return_sems, peer, peer
        )
        copy.wait_send()
        copy.wait_recv()
        return carry

    lax.fori_loop(1, groups, finish, 0)

    returned = jnp.concatenate([returned_ref[index] for index in range(groups)], axis=0).astype(
        jnp.bfloat16
    )
    kinds = 2 * cells
    picked_row = lax.broadcasted_iota(jnp.int32, (groups, groups * kinds), 1)
    channel_row = lax.broadcasted_iota(jnp.int32, (groups, groups * kinds), 0) * kinds

    def kind_of(cell, kind):
        picker = jnp.where(picked_row == channel_row + (2 * cell + kind), 1.0, 0.0)
        picked = jnp.dot(
            picker.astype(jnp.bfloat16), returned, preferred_element_type=jnp.float32
        )
        return (picked * live[cell]).astype(jnp.bfloat16)

    potentials = [kind_of(cell, 0) for cell in range(cells)]
    responses = [kind_of(cell, 1) for cell in range(cells)]
    gradient_in = jnp.zeros((groups, features_ref.shape[2]), jnp.float32)
    gradient_out = gradient_in
    for cell in range(cells):
        gradient_in = gradient_in + jnp.dot(
            responses[cell], features_ref[cell], preferred_element_type=jnp.float32
        )
        gradient_out = gradient_out + jnp.dot(
            potentials[cell], cotangent_ref[cell], preferred_element_type=jnp.float32
        )
    parts_ref[...] = placed_rows(
        [
            (0, gradient_in[:, :width]),
            (1, gradient_in[:, width:]),
            (2, gradient_out[:, :width]),
            (3, gradient_out[:, width:]),
        ],
        jnp.zeros(parts_ref.shape, jnp.float32),
    )

    def send_parts(step, carry):
        peer = lax.rem(own + step, groups)
        to_peer(
            parts_ref.at[peer], landed_ref.at[own], part_sems, land_sems, peer, own
        ).start()
        return carry

    lax.fori_loop(1, groups, send_parts, 0)
    for cell in range(cells):
        message_ref[cell] = lax.dot_general(
            potentials[cell],
            message_weight_ref[...],
            (((0,), (0,)), ((), ())),
            preferred_element_type=jnp.float32,
        ).astype(jnp.bfloat16)
        gradient_ref[cell] = lax.dot_general(
            responses[cell],
            charge_ref[...],
            (((0,), (0,)), ((), ())),
            preferred_element_type=jnp.float32,
        ).astype(jnp.bfloat16)
    row_index = lax.broadcasted_iota(jnp.int32, (8, width), 0)
    lane_index = lax.broadcasted_iota(jnp.int32, (8, width), 1)
    fixed = jnp.zeros((8, width), jnp.float32)
    for order_index in range(3):
        fixed = jnp.where(
            (row_index == 4) & (lane_index == order_index), own_terms[order_index], fixed
        )

    def gather_parts(step, total):
        peer = lax.rem(own + groups - step, groups)
        copy = to_peer(
            parts_ref.at[peer], landed_ref.at[peer], part_sems, land_sems, peer, peer
        )
        copy.wait_send()
        copy.wait_recv()
        return total + landed_ref[peer]

    totals_ref[own] = (
        lax.fori_loop(1, groups, gather_parts, parts_ref[own] + fixed) * gradient_scale
    )

    def spread_totals(step, carry):
        peer = lax.rem(own + step, groups)
        to_peer(
            totals_ref.at[own], totals_ref.at[own], spread_sems, total_sems, peer, own
        ).start()
        return carry

    lax.fori_loop(1, groups, spread_totals, 0)

    def finish_totals(step, carry):
        peer = lax.rem(own + groups - step, groups)
        copy = to_peer(
            totals_ref.at[own], totals_ref.at[peer], spread_sems, total_sems, peer, peer
        )
        copy.wait_send()
        copy.wait_recv()
        return carry

    lax.fori_loop(1, groups, finish_totals, 0)


def to_peer(source, target, send_sems, receive_sems, peer, sender):
    return pltpu.make_async_remote_copy(
        src_ref=source,
        dst_ref=target,
        send_sem=send_sems.at[peer],
        recv_sem=receive_sems.at[sender],
        device_id={"seq": peer},
        device_id_type=pl.DeviceIdType.MESH,
    )


def greet_peers(count, own):
    barrier = pltpu.get_barrier_semaphore()

    def greet(step, carry):
        pl.semaphore_signal(
            barrier,
            inc=1,
            device_id={"seq": lax.rem(own + step, count)},
            device_id_type=pl.DeviceIdType.MESH,
        )
        return carry

    lax.fori_loop(1, count, greet, 0)
    return barrier


def placed_rows(entries, base):
    row_index = lax.broadcasted_iota(jnp.int32, base.shape, 1)
    for row, table in entries:
        base = jnp.where(row_index == row, table[:, None, :], base)
    return base


def by_channel(
    atom_features,
    cotangent,
    charge_weight,
    message_weight,
    amplitude,
    smoothing,
    screening,
    base_cells,
    cell_offsets,
    row_starts,
    block_counts,
):
    cells, atoms, features = atom_features.shape
    groups = charge_weight.shape[1]
    planes = M // groups
    tables = stacked_tables(planes)
    sems = pltpu.SemaphoreType.DMA((groups,))
    whole = pl.BlockSpec(memory_space=pltpu.VMEM)
    scalar = pl.BlockSpec(memory_space=pltpu.SMEM)
    gradient_scale = 1.0 / math.sqrt(cells * atoms * groups)
    atom_blocks = (groups, cells, 8, atoms)
    value_blocks = (groups, 2 * cells, atoms)
    part_blocks = (groups, 8, 128)
    message, atom_gradient, totals = pl.pallas_call(
        functools.partial(mesh_kernel, planes, gradient_scale),
        out_shape=(
            jax.ShapeDtypeStruct(atom_features.shape, jnp.bfloat16),
            jax.ShapeDtypeStruct(atom_features.shape, jnp.bfloat16),
            jax.ShapeDtypeStruct(part_blocks, jnp.float32),
        ),
        in_specs=[scalar] * 4 + [whole] * 9,
        out_specs=(whole, whole, whole),
        scratch_shapes=[
            pltpu.VMEM(atom_blocks, jnp.float32),
            pltpu.VMEM(atom_blocks, jnp.float32),
            pltpu.VMEM(value_blocks, jnp.float32),
            pltpu.VMEM(value_blocks, jnp.float32),
            pltpu.VMEM(part_blocks, jnp.float32),
            pltpu.VMEM(part_blocks, jnp.float32),
            pltpu.VMEM((groups, cells, M * 8, atoms), jnp.bfloat16),
            pltpu.VMEM((groups, cells, M, atoms), jnp.float32),
            pltpu.VMEM((M, groups * 8, cells * 2 * M), jnp.float32),
            pltpu.VMEM((M, 2 * M), jnp.float32),
        ]
        + [sems] * 8,
        compiler_params=pltpu.CompilerParams(
            collective_id=0, has_side_effects=True, vmem_limit_bytes=56 * 1024 * 1024
        ),
    )(
        amplitude,
        smoothing,
        screening,
        block_counts,
        atom_features,
        cotangent,
        charge_weight.T,
        message_weight,
        jnp.swapaxes(base_cells, 0, 1),
        jnp.swapaxes(cell_offsets, 0, 1),
        *tables,
    )
    gradient_in = totals[:, 0:2].reshape(groups, features).T
    gradient_out = totals[:, 2:4].reshape(groups, features)
    filter_terms = totals[:, 4, :3].T
    return (message, atom_gradient, gradient_in, gradient_out, filter_terms)


def solution(mesh):

    def per_device(*arguments):
        by_channels = arguments[2].shape[1] == mesh.shape["seq"]
        return (by_channel if by_channels else on_device)(*arguments)

    in_specs = (
        P("groups", "seq", None),
        P("groups", "seq", None),
        P(),
        P(),
        P(),
        P(),
        P(),
        P("groups", None, "seq"),
        P("groups", None, "seq"),
        P("groups", "seq"),
        P("groups", "seq"),
    )
    out_specs = (
        P("groups", "seq", None),
        P("groups", "seq", None),
        P("groups", None),
        P("groups", None),
        P("groups", None),
    )
    return jax.shard_map(
        per_device, mesh=mesh, in_specs=in_specs, out_specs=out_specs, check_vma=False
    )
```

```python
import functools
import math

import jax
import jax.numpy as jnp
import ml_dtypes
import numpy as np
from jax import lax
from jax.experimental import pallas as pl
from jax.experimental.pallas import tpu as pltpu
from jax.sharding import PartitionSpec as P

M = 64
BAND = 32


def passed_along(value, axis, by):
    count = lax.axis_size(axis)
    return lax.ppermute(value, axis, [(i, (i + by) % count) for i in range(count)])


def spline_weights(fraction):
    remain = 1.0 - fraction
    square = fraction * fraction
    cubed = square * fraction
    return (
        remain * remain * remain / 6.0,
        (3.0 * cubed - 6.0 * square + 4.0) / 6.0,
        (-3.0 * cubed + 3.0 * square + 3.0 * fraction + 1.0) / 6.0,
        cubed / 6.0,
    )


def pick_weight(lattice_gap, weights):
    picked = jnp.where(lattice_gap == 0, weights[0], 0.0)
    for order_index in range(1, 4):
        picked = picked + jnp.where(lattice_gap == order_index, weights[order_index], 0.0)
    return picked


def atom_weights(base_cells, cell_offsets, row_start, plane_start, plane_count):
    atom_count = base_cells.shape[1]
    depth_index = plane_start + jnp.arange(plane_count, dtype=jnp.int32)
    row_index = row_start + jnp.arange(BAND, dtype=jnp.int32)
    column_index = jnp.arange(M, dtype=jnp.int32)
    along_depth = pick_weight(
        (depth_index[None, :] - base_cells[0][:, None]) % M,
        spline_weights(cell_offsets[0][:, None]),
    )
    along_rows = pick_weight(
        (row_index[None, :] - base_cells[1][:, None]) % M, spline_weights(cell_offsets[1][:, None])
    )
    along_columns = pick_weight(
        (column_index[None, :] - base_cells[2][:, None]) % M,
        spline_weights(cell_offsets[2][:, None]),
    )
    plane_rows = (
        (along_depth[:, :, None] * along_rows[:, None, :])
        .reshape(atom_count, plane_count * BAND)
        .astype(jnp.bfloat16)
    )
    return (plane_rows, along_columns)


def hartley_table():
    indices = jnp.arange(M, dtype=jnp.int32)
    product = indices[:, None] * indices[None, :] % M
    angles = product.astype(jnp.float32) * (2.0 * math.pi / M)
    return jnp.cos(angles) + jnp.sin(angles)


def wave_numbers(indices):
    return jnp.where(indices < M // 2, indices, indices - M).astype(jnp.float32) * (
        2.0 * math.pi / M
    )


def squared_waves(row_first, row_count):
    depth_waves = wave_numbers(jnp.arange(M, dtype=jnp.int32))
    row_waves = wave_numbers(row_first + jnp.arange(row_count, dtype=jnp.int32))
    summed = (
        depth_waves[:, None, None] ** 2
        + row_waves[None, :, None] ** 2
        + depth_waves[None, None, :] ** 2
    )
    return summed[:, :, None, :]


def scaled_filter(amplitude, smoothing, screening, wave_square):
    gains = amplitude[None, None, :, None]
    widths = (smoothing * smoothing)[None, None, :, None]
    screens = (screening * screening)[None, None, :, None]
    return gains * jnp.exp(-0.5 * widths * wave_square) / (wave_square + screens) * (1.0 / M**3)


def spread_cell(charges, base_cells, cell_offsets, row_starts, plane_start, plane_count):
    blocks = row_starts.shape[0]
    atom_count = charges.shape[0] // blocks
    columns = charges.shape[1] * M

    def add_block(padded, block_index):
        first_row = block_index * atom_count
        block_charges = lax.dynamic_slice_in_dim(charges, first_row, atom_count, 0)
        block_cells = lax.dynamic_slice_in_dim(base_cells, first_row, atom_count, 1)
        block_offsets = lax.dynamic_slice_in_dim(cell_offsets, first_row, atom_count, 1)
        row_start = row_starts[block_index]
        plane_rows, along_columns = atom_weights(
            block_cells, block_offsets, row_start, plane_start, plane_count
        )
        spread_rows = (
            (block_charges.astype(jnp.float32)[:, :, None] * along_columns[:, None, :])
            .reshape(atom_count, columns)
            .astype(jnp.bfloat16)
        )
        addition = lax.dot_general(
            plane_rows, spread_rows, (((0,), (0,)), ((), ())), preferred_element_type=jnp.float32
        )
        addition = addition.reshape(plane_count, BAND, columns)
        current = lax.dynamic_slice_in_dim(padded, row_start, BAND, 1)
        return (lax.dynamic_update_slice_in_dim(padded, current + addition, row_start, 1), None)

    padded = jnp.zeros((plane_count, M + BAND, columns), jnp.float32)
    padded, unused = lax.scan(add_block, padded, jnp.arange(blocks, dtype=jnp.int32))
    return padded[:, :M].at[:, :BAND].add(padded[:, M:])


def interpolate_cell(mesh, base_cells, cell_offsets, row_starts, plane_start):
    plane_count = mesh.shape[0]
    blocks = row_starts.shape[0]
    atom_count = base_cells.shape[1] // blocks
    padded = jnp.concatenate([mesh, mesh[:, :BAND]], axis=1)

    def one_block(block_index):
        first_row = block_index * atom_count
        block_cells = lax.dynamic_slice_in_dim(base_cells, first_row, atom_count, 1)
        block_offsets = lax.dynamic_slice_in_dim(cell_offsets, first_row, atom_count, 1)
        row_start = row_starts[block_index]
        plane_rows, along_columns = atom_weights(
            block_cells, block_offsets, row_start, plane_start, plane_count
        )
        window = lax.dynamic_slice_in_dim(padded, row_start, BAND, 1).reshape(
            plane_count * BAND, -1
        )
        values = jnp.dot(plane_rows, window, preferred_element_type=jnp.float32)
        return jnp.sum(values.reshape(atom_count, -1, M) * along_columns[:, None, :], axis=2)

    return lax.map(one_block, jnp.arange(blocks, dtype=jnp.int32)).reshape(blocks * atom_count, -1)


def spread_cells(charges, base_cells, cell_offsets, row_starts, plane_start, plane_count):

    def spread_one_cell(cell_data):
        return spread_cell(
            cell_data[0], cell_data[1], cell_data[2], cell_data[3], plane_start, plane_count
        )

    return lax.map(spread_one_cell, (charges, base_cells, cell_offsets, row_starts))


def interpolate_cells(mesh, base_cells, cell_offsets, row_starts, plane_start):

    def interpolate_one_cell(cell_data):
        return interpolate_cell(cell_data[0], cell_data[1], cell_data[2], cell_data[3], plane_start)

    return lax.map(interpolate_one_cell, (mesh, base_cells, cell_offsets, row_starts))


def long_range(charges, base_cells, cell_offsets, row_starts, spectral_filter):
    devices = lax.axis_size("seq")
    planes = M // devices
    spill_reach = (planes + 2) // planes
    plane_start = lax.axis_index("seq") * planes
    cell_count = charges.shape[0]
    channels = charges.shape[2]
    hartley = hartley_table()
    highest = lax.Precision.HIGHEST
    extended = spread_cells(charges, base_cells, cell_offsets, row_starts, plane_start, planes + 3)
    mesh_field = extended[:, :planes]
    for distance in range(1, spill_reach + 1):
        lower_plane = (distance - 1) * planes
        upper_plane = min(distance * planes, 3)
        arrived = passed_along(
            extended[:, planes + lower_plane : planes + upper_plane], "seq", distance
        )
        mesh_field = mesh_field.at[:, : upper_plane - lower_plane].add(arrived)
    slab_data = mesh_field.reshape(cell_count, planes, M, channels, M)
    spectrum = jnp.einsum("kpycx,xf->kpycf", slab_data, hartley, precision=highest)
    spectrum = jnp.einsum("kpycx,yf->kpfcx", spectrum, hartley, precision=highest)
    forward = jnp.einsum(
        "kzycx,zf->kfycx",
        lax.all_to_all(spectrum, "seq", split_axis=2, concat_axis=1, tiled=True),
        hartley,
        precision=highest,
    )
    weighted = spectral_filter[None] * forward
    returned = jnp.einsum("kzycx,zf->kfycx", weighted, hartley, precision=highest)
    slab_back = lax.all_to_all(returned, "seq", split_axis=1, concat_axis=2, tiled=True)
    slab_back = jnp.einsum("kpycx,yf->kpfcx", slab_back, hartley, precision=highest)
    slab_back = jnp.einsum("kpycx,xf->kpycf", slab_back, hartley, precision=highest)
    rounded = slab_back.reshape(cell_count, planes, M, channels * M).astype(jnp.bfloat16)
    pieces = [rounded]
    for distance in range(1, spill_reach + 1):
        lower_plane = (distance - 1) * planes
        upper_plane = min(distance * planes, 3)
        pieces.append(passed_along(rounded[:, : upper_plane - lower_plane], "seq", -distance))
    values = interpolate_cells(
        jnp.concatenate(pieces, axis=1), base_cells, cell_offsets, row_starts, plane_start
    )
    return (values, forward)


def on_device(
    atom_features,
    cotangent,
    charge_weight,
    message_weight,
    amplitude,
    smoothing,
    screening,
    base_cells,
    cell_offsets,
    row_starts,
    block_counts,
):
    cell_count, atom_rows, features = atom_features.shape
    channels = charge_weight.shape[1]
    devices = lax.axis_size("seq")
    blocks = block_counts.shape[1]
    slot_index = jnp.arange(atom_rows // blocks, dtype=jnp.int32)
    live_mask = (
        (slot_index[None, None, :] < block_counts[:, :, None])
        .reshape(cell_count, atom_rows)
        .astype(jnp.float32)
    )
    projected = jnp.dot(
        atom_features.reshape(-1, features), charge_weight, preferred_element_type=jnp.float32
    )
    charges = (live_mask[:, :, None] * projected.reshape(cell_count, atom_rows, channels)).astype(
        jnp.bfloat16
    )
    pulled = lax.dot_general(
        cotangent.reshape(-1, features),
        message_weight,
        (((1,), (1,)), ((), ())),
        preferred_element_type=jnp.float32,
    )
    adjoint = (live_mask[:, :, None] * pulled.reshape(cell_count, atom_rows, channels)).astype(
        jnp.bfloat16
    )
    row_count = M // devices
    wave_square = squared_waves(lax.axis_index("seq") * row_count, row_count)
    spectral_filter = scaled_filter(amplitude, smoothing, screening, wave_square)
    potential, source_spectra = long_range(
        charges, base_cells, cell_offsets, row_starts, spectral_filter
    )
    response, adjoint_spectra = long_range(
        adjoint, base_cells, cell_offsets, row_starts, spectral_filter
    )
    potential_rounded = potential.astype(jnp.bfloat16)
    outgoing = jnp.dot(
        potential_rounded.reshape(-1, channels), message_weight, preferred_element_type=jnp.float32
    )
    message = (live_mask[:, :, None] * outgoing.reshape(cell_count, atom_rows, features)).astype(
        jnp.bfloat16
    )
    response_rounded = (live_mask[:, :, None] * response).astype(jnp.bfloat16)
    backward = lax.dot_general(
        response_rounded.reshape(-1, channels),
        charge_weight,
        (((1,), (1,)), ((), ())),
        preferred_element_type=jnp.float32,
    )
    atom_gradient = backward.reshape(cell_count, atom_rows, features).astype(jnp.bfloat16)
    gradient_scale = 1.0 / math.sqrt(cell_count * atom_rows * devices)
    masked_cotangent = jnp.where(live_mask[:, :, None] > 0, cotangent, jnp.zeros((), jnp.bfloat16))
    gradient_in = (
        lax.dot_general(
            atom_features.reshape(-1, features),
            response_rounded.reshape(-1, channels),
            (((0,), (0,)), ((), ())),
            preferred_element_type=jnp.float32,
        )
        * gradient_scale
    )
    gradient_out = (
        lax.dot_general(
            potential_rounded.reshape(-1, channels),
            masked_cotangent.reshape(-1, features),
            (((0,), (0,)), ((), ())),
            preferred_element_type=jnp.float32,
        )
        * gradient_scale
    )
    intersection = jnp.sum(source_spectra * adjoint_spectra, axis=0) * spectral_filter
    widths = (smoothing * smoothing)[None, None, :, None]
    screens = (screening * screening)[None, None, :, None]
    smooth_factor = -widths * wave_square
    screen_factor = -2.0 * screens / (wave_square + screens)
    filter_terms = (
        jnp.stack(
            [
                jnp.sum(intersection, axis=(0, 1, 3)),
                jnp.sum(intersection * smooth_factor, axis=(0, 1, 3)),
                jnp.sum(intersection * screen_factor, axis=(0, 1, 3)),
            ]
        )
        * gradient_scale
    )
    gradient_in, gradient_out, filter_terms = lax.psum(
        (gradient_in, gradient_out, filter_terms), "seq"
    )
    return (message, atom_gradient, gradient_in, gradient_out, filter_terms)


def stacked_tables(planes):
    indices = np.arange(M)
    angles = (indices[:, None] * indices[None, :] % M) * (2.0 * np.pi / M)
    hartley = (np.cos(angles) + np.sin(angles)).astype(np.float32)
    window = (np.arange(M // planes)[:, None] * planes + np.arange(8)[None, :]) % M
    depth = hartley[:, window.reshape(-1)]

    def parts(table):
        high = table.astype(ml_dtypes.bfloat16)
        low = (table - high.astype(np.float32)).astype(ml_dtypes.bfloat16)
        return np.concatenate([high, high, low], axis=1)

    high, unused, low = np.split(parts(depth), 3, axis=1)
    stacked_depth = np.concatenate([high, low], axis=0)
    return tuple(jnp.asarray(table) for table in (parts(hartley), stacked_depth, parts(depth.T)))


def stacked_parts(value):
    high = value.astype(jnp.bfloat16)
    low = (value - high.astype(jnp.float32)).astype(jnp.bfloat16)
    return jnp.concatenate([high, low, high], axis=0)


def wave_squares(indices):
    waves = jnp.where(indices < M // 2, indices, indices - M).astype(jnp.float32)
    return waves * waves * ((2.0 * math.pi / M) ** 2)


def mesh_kernel(
    planes,
    gradient_scale,
    amplitude_ref,
    smoothing_ref,
    screening_ref,
    counts_ref,
    features_ref,
    cotangent_ref,
    charge_ref,
    message_weight_ref,
    bases_ref,
    offsets_ref,
    hartley_ref,
    depth_ref,
    back_ref,
    message_ref,
    gradient_ref,
    gradient_in_ref,
    gradient_out_ref,
    filter_ref,
    totals_ref,
    given_ref,
    atoms_ref,
    values_ref,
    returned_ref,
    parts_ref,
    landed_ref,
    atom_planes,
    atom_columns,
    mesh,
    plane_gains,
    send_sems,
    receive_sems,
    back_sems,
    return_sems,
    part_sems,
    land_sems,
    spread_sems,
    total_sems,
):
    groups, cells, unused, atoms = given_ref.shape
    blocks = counts_ref.shape[1]
    block_atoms = atoms // blocks
    width = 128
    lanes = 2 * M
    own = lax.axis_index("seq")
    barrier = greet_peers(groups, own)
    slot = lax.broadcasted_iota(jnp.int32, (1, atoms), 1)
    live = []
    for cell in range(cells):
        mask = jnp.zeros((1, atoms), jnp.float32)
        for block in range(blocks):
            first = block * block_atoms
            held = (slot >= first) & (slot < first + counts_ref[cell, block])
            mask = jnp.where(held, 1.0, mask)
        live.append(mask)
        projected = lax.dot_general(
            charge_ref[...],
            features_ref[cell],
            (((1,), (1,)), ((), ())),
            preferred_element_type=jnp.float32,
        )
        pulled = lax.dot_general(
            message_weight_ref[...],
            cotangent_ref[cell],
            (((1,), (1,)), ((), ())),
            preferred_element_type=jnp.float32,
        )
        places = jnp.concatenate(
            [
                *(bases_ref[way, cell : cell + 1].astype(jnp.float32) for way in range(3)),
                *(offsets_ref[way, cell : cell + 1] for way in range(3)),
                jnp.zeros((2, atoms), jnp.float32),
            ],
            axis=0,
        )
        given_ref[:, cell] = placed_rows(
            [
                (6, (projected * mask).astype(jnp.bfloat16).astype(jnp.float32)),
                (7, (pulled * mask).astype(jnp.bfloat16).astype(jnp.float32)),
            ],
            jnp.broadcast_to(places[None], (groups, 8, atoms)),
        )
    pl.semaphore_wait(barrier, groups - 1)

    def send_atoms(step, carry):
        peer = lax.rem(own + step, groups)
        to_peer(
            given_ref.at[peer], atoms_ref.at[own], send_sems, receive_sems, peer, own
        ).start()
        return carry

    lax.fori_loop(1, groups, send_atoms, 0)
    atoms_ref[own] = given_ref[own]

    def spread_group(group):
        for cell in range(cells):
            places = atoms_ref[group, cell]
            fractions = spline_weights(places[3:6])
            bases = places[0:3].astype(jnp.int32)
            window = lax.broadcasted_iota(jnp.int32, (8, atoms), 0)
            along_depth = pick_weight(
                window - (bases[0:1] - group * planes), [w[0:1] for w in fractions]
            )
            index = lax.broadcasted_iota(jnp.int32, (M, atoms), 0)
            along_rows = pick_weight((index - bases[1:2]) & (M - 1), [w[1:2] for w in fractions])
            along_columns = pick_weight(
                (index - bases[2:3]) & (M - 1), [w[2:3] for w in fractions]
            )
            both = jnp.concatenate(
                [stacked_parts(along_rows), stacked_parts(along_columns)], axis=1
            )
            waves = jnp.dot(hartley_ref[...], both, preferred_element_type=jnp.float32)
            row_waves = waves[:, :atoms]
            column_waves = waves[:, atoms:]
            plane_waves = (
                (row_waves[:, None, :] * along_depth[None, :, :])
                .reshape(M * 8, atoms)
                .astype(jnp.bfloat16)
            )
            terms = jnp.concatenate(
                [column_waves * places[6:7], column_waves * places[7:8]], axis=0
            ).astype(jnp.bfloat16)
            atom_planes[group, cell] = plane_waves
            atom_columns[group, cell] = column_waves
            added = lax.dot_general(
                plane_waves, terms, (((1,), (1,)), ((), ())), preferred_element_type=jnp.float32
            )
            mesh[:, pl.ds(pl.multiple_of(group * 8, 8), 8), cell * lanes : (cell + 1) * lanes] = (
                added.reshape(M, 8, lanes)
            )

    spread_group(own)
    together = 3 if groups % 3 == 1 else 1

    def spread_groups(step, carry):
        arrived = [
            lax.rem(own + groups - (1 + step * together + ahead), groups)
            for ahead in range(together)
        ]
        for group in arrived:
            to_peer(
                given_ref.at[group], atoms_ref.at[group], send_sems, receive_sems, group, group
            ).wait_recv()
        for group in arrived:
            spread_group(group)
        return carry

    lax.fori_loop(0, (groups - 1) // together, spread_groups, 0)

    amplitude = amplitude_ref[own]
    widths = smoothing_ref[own] * smoothing_ref[own]
    screens = screening_ref[own] * screening_ref[own]
    plane_squares = wave_squares(
        lax.broadcasted_iota(jnp.int32, (M, lanes), 0)
    ) + wave_squares(lax.broadcasted_iota(jnp.int32, (M, lanes), 1) & (M - 1))
    plane_gains[...] = (amplitude * (1.0 / M**3)) * jnp.exp((-0.5 * widths) * plane_squares)

    def filter_row(row, sums):
        both = jnp.dot(
            depth_ref[...], mesh[row].astype(jnp.bfloat16), preferred_element_type=jnp.float32
        )
        spectrum = both[:M] + both[M:]
        signed = jnp.where(row < M // 2, row, row - M).astype(jnp.float32)
        row_square = signed * signed * ((2.0 * math.pi / M) ** 2)
        squares = plane_squares + row_square
        screened = 1.0 / (squares + screens)
        row_gain = jnp.exp(jnp.full((1, lanes), (-0.5 * widths) * row_square, jnp.float32))
        gains = plane_gains[...] * row_gain * screened
        crossed = jnp.zeros((M, lanes), jnp.float32)
        filtered = []
        for cell in range(cells):
            part = spectrum[:, cell * lanes : (cell + 1) * lanes]
            crossed = crossed + part * pltpu.roll(part, M, 1)
            filtered.append(part * gains)
        crossed = crossed * gains
        mesh[row] = jnp.dot(
            back_ref[...],
            stacked_parts(jnp.concatenate(filtered, axis=1)),
            preferred_element_type=jnp.float32,
        )
        pieces = (crossed, crossed * squares, crossed * screened)
        return tuple(
            total + jnp.sum(piece.reshape(M // 8, 8, lanes), axis=0)
            for total, piece in zip(sums, pieces)
        )

    zero = jnp.zeros((8, lanes), jnp.float32)
    sums = lax.fori_loop(0, M, filter_row, (zero, zero, zero), unroll=16)
    own_terms = [
        jnp.sum(jnp.sum(total, axis=0, keepdims=True), axis=1, keepdims=True) * factor
        for total, factor in zip(sums, (0.5, -0.5 * widths, -screens))
    ]

    def read_group(group):
        for cell in range(cells):
            window = (
                mesh[
                    :, pl.ds(pl.multiple_of(group * 8, 8), 8), cell * lanes : (cell + 1) * lanes
                ]
                .reshape(M * 8, lanes)
                .astype(jnp.bfloat16)
            )
            inner = lax.dot_general(
                window,
                atom_planes[group, cell],
                (((0,), (0,)), ((), ())),
                preferred_element_type=jnp.float32,
            )
            weighted = inner.reshape(2, M, atoms) * atom_columns[group, cell][None]
            values_ref[group, 2 * cell : 2 * cell + 2] = jnp.sum(weighted, axis=1)

    def read_groups(step, carry):
        asked = [
            lax.rem(own + (1 + step * together + ahead), groups) for ahead in range(together)
        ]
        for group in asked:
            read_group(group)
        for group in asked:
            to_peer(
                values_ref.at[group], returned_ref.at[own], back_sems, return_sems, group, own
            ).start()
        return carry

    lax.fori_loop(0, (groups - 1) // together, read_groups, 0)
    read_group(own)
    returned_ref[own] = values_ref[own]

    def finish(step, carry):
        peer = lax.rem(own + groups - step, groups)
        to_peer(
            given_ref.at[peer], atoms_ref.at[peer], send_sems, receive_sems, peer, peer
        ).wait_send()
        copy = to_peer(
            values_ref.at[peer], returned_ref.at[peer], back_sems, return_sems, peer, peer
        )
        copy.wait_send()
        copy.wait_recv()
        return carry

    lax.fori_loop(1, groups, finish, 0)

    returned = jnp.concatenate([returned_ref[index] for index in range(groups)], axis=0).astype(
        jnp.bfloat16
    )
    kinds = 2 * cells
    picked_row = lax.broadcasted_iota(jnp.int32, (groups, groups * kinds), 1)
    channel_row = lax.broadcasted_iota(jnp.int32, (groups, groups * kinds), 0) * kinds

    def kind_of(cell, kind):
        picker = jnp.where(picked_row == channel_row + (2 * cell + kind), 1.0, 0.0)
        picked = jnp.dot(
            picker.astype(jnp.bfloat16), returned, preferred_element_type=jnp.float32
        )
        return (picked * live[cell]).astype(jnp.bfloat16)

    potentials = [kind_of(cell, 0) for cell in range(cells)]
    responses = [kind_of(cell, 1) for cell in range(cells)]
    gradient_in = jnp.zeros((groups, features_ref.shape[2]), jnp.float32)
    gradient_out = gradient_in
    for cell in range(cells):
        gradient_in = gradient_in + jnp.dot(
            responses[cell], features_ref[cell], preferred_element_type=jnp.float32
        )
        gradient_out = gradient_out + jnp.dot(
            potentials[cell], cotangent_ref[cell], preferred_element_type=jnp.float32
        )
    parts_ref[...] = placed_rows(
        [
            (0, gradient_in[:, :width]),
            (1, gradient_in[:, width:]),
            (2, gradient_out[:, :width]),
            (3, gradient_out[:, width:]),
        ],
        jnp.zeros(parts_ref.shape, jnp.float32),
    )

    def send_parts(step, carry):
        peer = lax.rem(own + step, groups)
        to_peer(
            parts_ref.at[peer], landed_ref.at[own], part_sems, land_sems, peer, own
        ).start()
        return carry

    lax.fori_loop(1, groups, send_parts, 0)
    for cell in range(cells):
        message_ref[cell] = lax.dot_general(
            potentials[cell],
            message_weight_ref[...],
            (((0,), (0,)), ((), ())),
            preferred_element_type=jnp.float32,
        ).astype(jnp.bfloat16)
        gradient_ref[cell] = lax.dot_general(
            responses[cell],
            charge_ref[...],
            (((0,), (0,)), ((), ())),
            preferred_element_type=jnp.float32,
        ).astype(jnp.bfloat16)
    row_index = lax.broadcasted_iota(jnp.int32, (8, width), 0)
    lane_index = lax.broadcasted_iota(jnp.int32, (8, width), 1)
    fixed = jnp.zeros((8, width), jnp.float32)
    for order_index in range(3):
        fixed = jnp.where(
            (row_index == 4) & (lane_index == order_index), own_terms[order_index], fixed
        )

    def gather_parts(step, total):
        peer = lax.rem(own + groups - step, groups)
        copy = to_peer(
            parts_ref.at[peer], landed_ref.at[peer], part_sems, land_sems, peer, peer
        )
        copy.wait_send()
        copy.wait_recv()
        return total + landed_ref[peer]

    totals_ref[own] = (
        lax.fori_loop(1, groups, gather_parts, parts_ref[own] + fixed) * gradient_scale
    )

    def spread_totals(step, carry):
        peer = lax.rem(own + step, groups)
        to_peer(
            totals_ref.at[own], totals_ref.at[own], spread_sems, total_sems, peer, own
        ).start()
        return carry

    lax.fori_loop(1, groups, spread_totals, 0)

    def finish_totals(step, carry):
        peer = lax.rem(own + groups - step, groups)
        copy = to_peer(
            totals_ref.at[own], totals_ref.at[peer], spread_sems, total_sems, peer, peer
        )
        copy.wait_send()
        copy.wait_recv()
        return carry

    lax.fori_loop(1, groups, finish_totals, 0)
    gradient_in_ref[:, :width] = totals_ref[:, 0, :]
    gradient_in_ref[:, width:] = totals_ref[:, 1, :]
    gradient_out_ref[:, :width] = totals_ref[:, 2, :]
    gradient_out_ref[:, width:] = totals_ref[:, 3, :]
    filter_ref[...] = totals_ref[:, 4, :]


def to_peer(source, target, send_sems, receive_sems, peer, sender):
    return pltpu.make_async_remote_copy(
        src_ref=source,
        dst_ref=target,
        send_sem=send_sems.at[peer],
        recv_sem=receive_sems.at[sender],
        device_id={"seq": peer},
        device_id_type=pl.DeviceIdType.MESH,
    )


def greet_peers(count, own):
    barrier = pltpu.get_barrier_semaphore()

    def greet(step, carry):
        pl.semaphore_signal(
            barrier,
            inc=1,
            device_id={"seq": lax.rem(own + step, count)},
            device_id_type=pl.DeviceIdType.MESH,
        )
        return carry

    lax.fori_loop(1, count, greet, 0)
    return barrier


def placed_rows(entries, base):
    row_index = lax.broadcasted_iota(jnp.int32, base.shape, 1)
    for row, table in entries:
        base = jnp.where(row_index == row, table[:, None, :], base)
    return base


def by_channel(
    atom_features,
    cotangent,
    charge_weight,
    message_weight,
    amplitude,
    smoothing,
    screening,
    base_cells,
    cell_offsets,
    row_starts,
    block_counts,
):
    cells, atoms, features = atom_features.shape
    groups = charge_weight.shape[1]
    planes = M // groups
    tables = stacked_tables(planes)
    sems = pltpu.SemaphoreType.DMA((groups,))
    whole = pl.BlockSpec(memory_space=pltpu.VMEM)
    scalar = pl.BlockSpec(memory_space=pltpu.SMEM)
    gradient_scale = 1.0 / math.sqrt(cells * atoms * groups)
    atom_blocks = (groups, cells, 8, atoms)
    value_blocks = (groups, 2 * cells, atoms)
    part_blocks = (groups, 8, 128)
    message, atom_gradient, gradient_in, gradient_out, filter_rows = pl.pallas_call(
        functools.partial(mesh_kernel, planes, gradient_scale),
        out_shape=(
            jax.ShapeDtypeStruct(atom_features.shape, jnp.bfloat16),
            jax.ShapeDtypeStruct(atom_features.shape, jnp.bfloat16),
            jax.ShapeDtypeStruct((groups, features), jnp.float32),
            jax.ShapeDtypeStruct((groups, features), jnp.float32),
            jax.ShapeDtypeStruct((groups, 128), jnp.float32),
        ),
        in_specs=[scalar] * 4 + [whole] * 9,
        out_specs=(whole,) * 5,
        scratch_shapes=[
            pltpu.VMEM(part_blocks, jnp.float32),
            pltpu.VMEM(atom_blocks, jnp.float32),
            pltpu.VMEM(atom_blocks, jnp.float32),
            pltpu.VMEM(value_blocks, jnp.float32),
            pltpu.VMEM(value_blocks, jnp.float32),
            pltpu.VMEM(part_blocks, jnp.float32),
            pltpu.VMEM(part_blocks, jnp.float32),
            pltpu.VMEM((groups, cells, M * 8, atoms), jnp.bfloat16),
            pltpu.VMEM((groups, cells, M, atoms), jnp.float32),
            pltpu.VMEM((M, groups * 8, cells * 2 * M), jnp.float32),
            pltpu.VMEM((M, 2 * M), jnp.float32),
        ]
        + [sems] * 8,
        compiler_params=pltpu.CompilerParams(
            collective_id=0, has_side_effects=True, vmem_limit_bytes=56 * 1024 * 1024
        ),
    )(
        amplitude,
        smoothing,
        screening,
        block_counts,
        atom_features,
        cotangent,
        charge_weight.T,
        message_weight,
        jnp.swapaxes(base_cells, 0, 1),
        jnp.swapaxes(cell_offsets, 0, 1),
        *tables,
    )
    return (message, atom_gradient, gradient_in.T, gradient_out, filter_rows[:, :3].T)


def solution(mesh):

    def per_device(*arguments):
        by_channels = arguments[2].shape[1] == mesh.shape["seq"]
        return (by_channel if by_channels else on_device)(*arguments)

    in_specs = (
        P("groups", "seq", None),
        P("groups", "seq", None),
        P(),
        P(),
        P(),
        P(),
        P(),
        P("groups", None, "seq"),
        P("groups", None, "seq"),
        P("groups", "seq"),
        P("groups", "seq"),
    )
    out_specs = (
        P("groups", "seq", None),
        P("groups", "seq", None),
        P("groups", None),
        P("groups", None),
        P("groups", None),
    )
    return jax.shard_map(
        per_device, mesh=mesh, in_specs=in_specs, out_specs=out_specs, check_vma=False
    )
```
